32 devices in a mesh: parts: 2 (over x), grid: 16 (over z, y, core).
Axes of the slice: x: 2, y: 2, z: 4, core: 2. Of those that a mesh axis runs over, the one named last changes fastest.
Arguments:
- block_values: bfloat16 [96, 8, 256, 256], P(('parts', 'grid')), parts along dimension 0, may hold values from -0.59765625 to 0.59765625
- pattern: int32 [96, 8], P('parts'), parts along dimension 0, may hold values from 0 to 47, as said below
Outputs:
- purified: bfloat16 [96, 8, 256, 256], P(('parts', 'grid')), parts along dimension 0
The draws below stay inside these ranges and needn't reach their ends.
There are 2 independent parts, one for each index of `parts`. The reference program is written for one: setup_inputs(seed, part) draws one part's arguments, and reference() takes and returns one part's arrays. A program takes and returns all parts, laid end to end along the dimension named above; each array names one. Nothing has to cross between parts.
Inputs may be any that keep to these rules, and one draw needn't show every extreme that they name: `pattern`: within a row the 8 columns are distinct and include the row's own index; row i, on device d = i // 3, names only block rows of devices d - 1 to d + 1, counted cyclically over 48 block rows.
All inputs are finite; a program needn't handle non-finite values.
Results may differ from the reference program's by a relative error of at most 0.0049.
Values may be sent and summed in bfloat16 or wider, within the bound.
No kernel may reach another device: no remote copies, remote signals or barrier semaphores. Data moves between devices by JAX's collectives and lax.ppermute only.
A program may use at most 128 MiB of HBM per device.

```python
import jax
import jax.numpy as jnp
from jax import lax

BS = 256
RB = 3
KB = 8
REACH = 1
NB = 48


def draw_pattern(key, part):
    key = jax.random.fold_in(key, 7)
    span = (2 * REACH + 1) * RB
    offsets = jnp.arange(span, dtype=jnp.int32)
    scores = jax.random.randint(key, (NB, span), 0, 1 << 20, dtype=jnp.int32) * span + offsets[None, :]
    row_ids = jnp.arange(NB, dtype=jnp.int32)
    diagonal = REACH * RB + row_ids % RB
    scores = jnp.where(offsets[None, :] == diagonal[:, None], -1, scores)
    chosen = jnp.argsort(scores, axis=1)[:, :KB].astype(jnp.int32)
    first = (row_ids // RB - REACH) * RB
    return ((first[:, None] + chosen) % NB).astype(jnp.int32)


def steps_of(rng, extent, pieces, low, top_value):
    loudness = 1.0
    for dim, parts in pieces:
        heights = jax.random.uniform(jax.random.fold_in(jax.random.fold_in(rng, 6), dim), (parts,), jnp.float32, low / len(pieces), top_value / len(pieces))
        loudness = loudness * jnp.repeat(jnp.exp(heights), extent[dim] // parts).reshape((-1,) + (1,) * (len(extent) - 1 - dim))
    return loudness


def noise(rng, dims, spread, bound, cuts=(), kind=jnp.bfloat16):
    array = jax.random.normal(rng, dims, jnp.float32) * spread
    if len(cuts) > 0:
        array = steps_of(rng, dims, cuts, -0.22, 0.18) * array
    return jnp.clip(array, min=-bound, max=bound).astype(kind)


def setup_inputs(seed: int = 0, part: int = 0) -> dict:
    seeds = jax.random.split(jax.random.key(seed), 3)
    own_keys = jax.random.split(jax.random.fold_in(seeds[2], part), 3)
    return {
        "block_values": noise(own_keys[0], (NB, KB, BS, BS), 0.1, 0.59765625, ((0, 16),)),
        "pattern": draw_pattern(jax.random.fold_in(jax.random.fold_in(seeds[2], part), 71), part),
    }


def filtered_product(left_blocks, right_blocks, pattern):
    total_rows = pattern.shape[0]

    def one_row(row_index):
        own_cols = pattern[row_index]
        picked = right_blocks[own_cols].astype(jnp.float32)
        inner = pattern[own_cols]
        matches = (inner[:, :, None] == own_cols[None, None, :]).astype(jnp.float32)
        chosen = jnp.einsum("qst,qsyz->qtyz", matches, picked)
        chosen = chosen.astype(jnp.bfloat16).astype(jnp.float32)
        return jnp.einsum("qxy,qtyz->txz", left_blocks[row_index].astype(jnp.float32), chosen)

    return lax.map(one_row, jnp.arange(total_rows, dtype=jnp.int32))


def reference(block_values, pattern):
    square = filtered_product(block_values, block_values, pattern).astype(jnp.bfloat16)
    cube = filtered_product(block_values, square, pattern)
    return (3.0 * square.astype(jnp.float32) - 2.0 * cube).astype(jnp.bfloat16)
```

```python
import functools

import jax
import jax.numpy as jnp
from jax import lax
from jax.experimental import pallas as pl
from jax.experimental.pallas import tpu as pltpu
from jax.sharding import PartitionSpec as P


F32 = jnp.float32
BF16 = jnp.bfloat16
ANY = pl.BlockSpec(memory_space=pl.ANY)
HBM = pl.BlockSpec(memory_space=pltpu.HBM)
VMEM = pl.BlockSpec(memory_space=pltpu.VMEM)
SMEM = pl.BlockSpec(memory_space=pltpu.SMEM)
VMEM_LIMIT = 40 * 1024 * 1024


def neighbours(devices):
    me = lax.axis_index("grid")
    odd = lax.rem(me, 2)
    above = lax.rem(me + 1, devices)
    below = lax.rem(me + devices - 1, devices)
    return me, jnp.where(odd == 1, above, below), jnp.where(odd == 1, below, above)


def slot_of(pattern, row, column):
    slot = jnp.int32(-1)
    for s in range(pattern.shape[1]):
        slot = jnp.where(pattern[row, s] == column, s, slot)
    return slot


def panel_product(left, right, c, rb, bs):
    total = jnp.dot(left[0], right[c, pl.ds(0, bs), :], preferred_element_type=F32)
    for k in range(1, rb):
        total += jnp.dot(left[k], right[c, pl.ds(k * bs, bs), :], preferred_element_type=F32)
    return total


def drop_absent(ref, pattern, row_device, column_device, rb, bs):
    for r in range(rb):
        for j in range(rb):
            slot = slot_of(pattern, row_device * rb + r, column_device * rb + j)

            @pl.when(slot < 0)
            def _():
                ref[j, pl.ds(r * bs, bs), :] = jnp.zeros((bs, bs), ref.dtype)


def pack_kernel(devices, rb, bs, pattern_hbm, blocks, *rest):
    cuts, (pattern, held, zeros, pattern_sem, in_sems, out_sems) = rest[:3], rest[3:]
    fetch = pltpu.make_async_copy(pattern_hbm, pattern, pattern_sem)
    fetch.start()
    loads = [pltpu.make_async_copy(blocks.at[r], held.at[r], in_sems.at[r]) for r in range(rb)]
    for load in loads:
        load.start()
    zeros[...] = jnp.zeros_like(zeros)
    people = neighbours(devices)
    me = people[0]
    fetch.wait()
    stores = []
    for n, (column_device, out) in enumerate(zip((people[1], me, people[2]), cuts)):
        for r in range(rb):
            if n == 0:
                loads[r].wait()
            for j in range(rb):
                slot = slot_of(pattern, me * rb + r, column_device * rb + j)
                sem = out_sems.at[(n * rb + r) * rb + j]
                dst = out.at[j, pl.ds(r * bs, bs), :]
                found = pltpu.make_async_copy(held.at[r, jnp.maximum(slot, 0)], dst, sem)
                absent = pltpu.make_async_copy(zeros, dst, sem)
                pl.when(slot >= 0)(found.start)
                pl.when(slot < 0)(absent.start)
                stores.append(absent)
    for store in stores:
        store.wait()


def pack(devices, pattern, blocks):
    rb, _, bs, _ = blocks.shape
    return pl.pallas_call(
        functools.partial(pack_kernel, devices, rb, bs),
        out_shape=[jax.ShapeDtypeStruct((rb, rb * bs, bs), blocks.dtype)] * 3,
        in_specs=[HBM, HBM],
        out_specs=[ANY] * 3,
        scratch_shapes=[
            pltpu.SMEM(pattern.shape, pattern.dtype),
            pltpu.VMEM(blocks.shape, blocks.dtype),
            pltpu.VMEM((bs, bs), blocks.dtype),
            pltpu.SemaphoreType.DMA,
            pltpu.SemaphoreType.DMA((rb,)),
            pltpu.SemaphoreType.DMA((3 * rb * rb,)),
        ],
        compiler_params=pltpu.CompilerParams(vmem_limit_bytes=VMEM_LIMIT),
        cost_estimate=pl.CostEstimate(
            flops=0, bytes_accessed=6 * rb * rb * bs * bs * 2, transcendentals=0
        ),
        name="pack",
    )(pattern, blocks)


def call(kernel, devices, rb, bs, products, operands, out_dtypes, name, **more):
    cut = (rb, rb * bs, bs)
    return pl.pallas_call(
        functools.partial(kernel, devices, rb, bs),
        out_shape=[jax.ShapeDtypeStruct(cut, t) for t in out_dtypes],
        in_specs=[SMEM] + [VMEM] * (len(operands) - 1),
        out_specs=[VMEM] * len(out_dtypes),
        compiler_params=pltpu.CompilerParams(vmem_limit_bytes=VMEM_LIMIT),
        cost_estimate=pl.CostEstimate(
            flops=products * 2 * (rb * bs) ** 3,
            bytes_accessed=(len(operands) + len(out_dtypes)) * rb * rb * bs * bs * 2,
            transcendentals=0,
        ),
        name=name,
        **more,
    )(*operands)


def inner_kernel(devices, rb, bs, pattern, own, inner, from_inner, inner_own, s_inner, s_from_inner, part):
    me, _, partner = neighbours(devices)

    @pl.loop(0, rb)
    def _(c):
        s_inner[c] = (panel_product(own, inner, c, rb, bs) + panel_product(inner, inner_own, c, rb, bs)).astype(BF16)
        s_from_inner[c] = (
            panel_product(from_inner, own, c, rb, bs) + panel_product(inner_own, from_inner, c, rb, bs)
        ).astype(BF16)
        part[c] = panel_product(own, own, c, rb, bs) + panel_product(inner, from_inner, c, rb, bs)

    drop_absent(s_inner, pattern, me, partner, rb, bs)
    drop_absent(s_from_inner, pattern, partner, me, rb, bs)


def own_kernel(devices, rb, bs, pattern, outer, from_outer, part, s_own):
    me, _, _ = neighbours(devices)

    @pl.loop(0, rb)
    def _(c):
        s_own[c] = (part[c] + panel_product(outer, from_outer, c, rb, bs)).astype(BF16)

    drop_absent(s_own, pattern, me, me, rb, bs)


def scatter(out, pattern, me, column_device, panels, sems, base, rb, bs):
    waits = []
    for r in range(rb):
        for j in range(rb):
            slot = slot_of(pattern, me * rb + r, column_device * rb + j)
            copy = pltpu.make_async_copy(
                panels.at[j, pl.ds(r * bs, bs), :],
                out.at[r, jnp.maximum(slot, 0)],
                sems.at[base + r * rb + j],
            )
            pl.when(slot >= 0)(copy.start)
            waits.append((slot, copy))
    return waits


def settle(waits):
    for slot, copy in waits:
        pl.when(slot >= 0)(copy.wait)


def middle_kernel(
    devices, rb, bs, pattern, own, outer, inner, outer_own, from_outer, s_own, s_inner, s_from_inner, s_inner_own,
    out, rest, s_outer, s_from_outer, out_own, out_inner, sems,
):
    me, other, partner = neighbours(devices)

    @pl.loop(0, rb)
    def _(c):
        out_inner[c] = (
            3.0 * s_inner[c].astype(F32)
            - 2.0 * (panel_product(own, s_inner, c, rb, bs) + panel_product(inner, s_inner_own, c, rb, bs))
        ).astype(BF16)

    waits = scatter(out, pattern, me, partner, out_inner, sems, 0, rb, bs)

    @pl.loop(0, rb)
    def _(c):
        s_outer[c] = (panel_product(own, outer, c, rb, bs) + panel_product(outer, outer_own, c, rb, bs)).astype(BF16)
        s_from_outer[c] = (
            panel_product(from_outer, own, c, rb, bs) + panel_product(outer_own, from_outer, c, rb, bs)
        ).astype(BF16)

    drop_absent(s_outer, pattern, me, other, rb, bs)
    drop_absent(s_from_outer, pattern, other, me, rb, bs)

    @pl.loop(0, rb)
    def _(c):
        rest[c] = 3.0 * s_outer[c].astype(F32) - 2.0 * panel_product(own, s_outer, c, rb, bs)
        cube = panel_product(own, s_own, c, rb, bs)
        cube += panel_product(outer, s_from_outer, c, rb, bs)
        cube += panel_product(inner, s_from_inner, c, rb, bs)
        out_own[c] = (3.0 * s_own[c].astype(F32) - 2.0 * cube).astype(BF16)

    waits += scatter(out, pattern, me, me, out_own, sems, rb * rb, rb, bs)
    settle(waits)


def last_kernel(devices, rb, bs, pattern, outer, s_outer_own, rest, _, out, panels, sems):
    me, other, _ = neighbours(devices)

    @pl.loop(0, rb)
    def _(c):
        panels[c] = (rest[c] - 2.0 * panel_product(outer, s_outer_own, c, rb, bs)).astype(BF16)

    settle(scatter(out, pattern, me, other, panels, sems, 0, rb, bs))


def local(devices, block_values, pattern):
    rb, _, bs, _ = block_values.shape
    cut = (rb, rb * bs, bs)
    one = 2 * rb * rb * bs * bs
    over = [(i, (i + 1 if i % 2 else i - 1) % devices) for i in range(devices)]
    across = [(i, i ^ 1) for i in range(devices)]
    to_outer = lambda x: lax.ppermute(x, "grid", over)
    to_inner = lambda x: lax.ppermute(x, "grid", across)

    outer, own, inner = pack(devices, pattern, block_values)
    from_outer = to_outer(outer)
    outer_own = to_outer(own)
    from_inner, inner_own = to_inner(inner), to_inner(own)

    s_inner, s_from_inner, part = call(
        inner_kernel, devices, rb, bs, 6, (pattern, own, inner, from_inner, inner_own), (BF16, BF16, F32), "inner"
    )
    (s_own,) = call(own_kernel, devices, rb, bs, 1, (pattern, outer, from_outer, part), (BF16,), "square")
    s_outer_own = to_outer(s_own)
    s_inner_own = to_inner(s_own)

    operands = (pattern, own, outer, inner, outer_own, from_outer, s_own, s_inner, s_from_inner, s_inner_own)
    out, rest = pl.pallas_call(
        functools.partial(middle_kernel, devices, rb, bs),
        out_shape=[jax.ShapeDtypeStruct(block_values.shape, BF16), jax.ShapeDtypeStruct(cut, F32)],
        in_specs=[SMEM] + [VMEM] * 9,
        out_specs=[ANY, VMEM],
        scratch_shapes=[pltpu.VMEM(cut, BF16)] * 4 + [pltpu.SemaphoreType.DMA((2 * rb * rb,))],
        compiler_params=pltpu.CompilerParams(vmem_limit_bytes=VMEM_LIMIT),
        cost_estimate=pl.CostEstimate(
            flops=10 * 2 * (rb * bs) ** 3, bytes_accessed=13 * one, transcendentals=0
        ),
        name="middle",
    )(*operands)
    return pl.pallas_call(
        functools.partial(last_kernel, devices, rb, bs),
        out_shape=jax.ShapeDtypeStruct(block_values.shape, BF16),
        in_specs=[SMEM] + [VMEM] * 3 + [ANY],
        out_specs=ANY,
        input_output_aliases={4: 0},
        scratch_shapes=[pltpu.VMEM(cut, BF16), pltpu.SemaphoreType.DMA((rb * rb,))],
        compiler_params=pltpu.CompilerParams(vmem_limit_bytes=VMEM_LIMIT),
        cost_estimate=pl.CostEstimate(flops=2 * (rb * bs) ** 3, bytes_accessed=5 * one, transcendentals=0),
        name="last",
    )(pattern, outer, s_outer_own, rest, out)


def solution(mesh):
    return jax.shard_map(
        functools.partial(local, mesh.shape["grid"]),
        mesh=mesh,
        in_specs=(P(("parts", "grid"), None, None, None), P("parts", None)),
        out_specs=P(("parts", "grid"), None, None, None),
        check_vma=False,
    )
```

```python
import functools

import jax
import jax.numpy as jnp
from jax import lax
from jax.experimental import pallas as pl
from jax.experimental.pallas import tpu as pltpu
from jax.sharding import PartitionSpec as P


F32 = jnp.float32
BF16 = jnp.bfloat16
ANY = pl.BlockSpec(memory_space=pl.ANY)
HBM = pl.BlockSpec(memory_space=pltpu.HBM)
VMEM = pl.BlockSpec(memory_space=pltpu.VMEM)
SMEM = pl.BlockSpec(memory_space=pltpu.SMEM)
BRIEF = pl.CostEstimate(flops=1, bytes_accessed=1, transcendentals=0)
VMEM_LIMIT = 24 * 1024 * 1024


def neighbours(devices):
    me = lax.axis_index("grid")
    odd = lax.rem(me, 2)
    above = lax.rem(me + 1, devices)
    below = lax.rem(me + devices - 1, devices)
    return me, jnp.where(odd == 1, above, below), jnp.where(odd == 1, below, above)


def slot_of(pattern, row, column):
    slot = jnp.int32(-1)
    for s in range(pattern.shape[0]):
        slot = jnp.where(pattern[s, row] == column, s, slot)
    return slot


def panel_product(left, right, c, rb, bs):
    total = jnp.dot(left[0], right[c, pl.ds(0, bs), :], preferred_element_type=F32)
    for k in range(1, rb):
        total += jnp.dot(left[k], right[c, pl.ds(k * bs, bs), :], preferred_element_type=F32)
    return total


def drop_absent(ref, pattern, row_device, column_device, rb, bs):
    for r in range(rb):
        for j in range(rb):
            slot = slot_of(pattern, row_device * rb + r, column_device * rb + j)

            @pl.when(slot < 0)
            def _():
                ref[j, pl.ds(r * bs, bs), :] = jnp.zeros((bs, bs), ref.dtype)


def pack_kernel(devices, rb, bs, pattern_hbm, blocks, *rest):
    cuts, (pattern, held, pattern_sem, sems) = rest[:3], rest[3:]
    fetch = pltpu.make_async_copy(pattern_hbm, pattern, pattern_sem)
    fetch.start()
    loads = [pltpu.make_async_copy(blocks.at[r], held.at[r], sems.at[r]) for r in range(rb)]
    for load in loads:
        load.start()
    me, other, partner = neighbours(devices)
    fetch.wait()
    for r in range(rb):
        slots = [
            [slot_of(pattern, me * rb + r, column_device * rb + j) for j in range(rb)]
            for column_device in (other, me, partner)
        ]
        loads[r].wait()
        for cut, row in zip(cuts, slots):
            for j, slot in enumerate(row):
                block = held[r, jnp.maximum(slot, 0)]
                cut[j, pl.ds(r * bs, bs), :] = jnp.where(slot >= 0, block, jnp.zeros_like(block))


def pack(devices, pattern, blocks):
    rb, _, bs, _ = blocks.shape
    return pl.pallas_call(
        functools.partial(pack_kernel, devices, rb, bs),
        out_shape=[jax.ShapeDtypeStruct((rb, rb * bs, bs), blocks.dtype)] * 3,
        in_specs=[ANY, ANY],
        out_specs=[VMEM] * 3,
        scratch_shapes=[
            pltpu.SMEM(pattern.shape, pattern.dtype),
            pltpu.VMEM(blocks.shape, blocks.dtype),
            pltpu.SemaphoreType.DMA,
            pltpu.SemaphoreType.DMA((rb,)),
        ],
        compiler_params=pltpu.CompilerParams(vmem_limit_bytes=VMEM_LIMIT),
        cost_estimate=BRIEF,
        name="pack",
    )(
        pltpu.with_memory_space_constraint(pattern, pltpu.HBM),
        pltpu.with_memory_space_constraint(blocks, pltpu.HBM),
    )


def scatter(out, pattern, me, column_device, panels, j, sems, base, rb, bs):
    waits = []
    for r in range(rb):
        slot = slot_of(pattern, me * rb + r, column_device * rb + j)
        copy = pltpu.make_async_copy(
            panels.at[j, pl.ds(r * bs, bs), :], out.at[r, jnp.maximum(slot, 0)], sems.at[base + r * rb + j]
        )
        pl.when(slot >= 0)(copy.start)
        waits.append((slot, copy))
    return waits


def settle(waits):
    for slot, copy in waits:
        pl.when(slot >= 0)(copy.wait)


def inner_kernel(
    devices, rb, bs, pattern, own, inner, outer, from_inner, inner_own, s_inner, s_from_inner, own_part, outer_part
):
    me, _, partner = neighbours(devices)

    @pl.loop(0, rb)
    def _(c):
        s_inner[c] = (panel_product(own, inner, c, rb, bs) + panel_product(inner, inner_own, c, rb, bs)).astype(BF16)
        s_from_inner[c] = (
            panel_product(from_inner, own, c, rb, bs) + panel_product(inner_own, from_inner, c, rb, bs)
        ).astype(BF16)
        own_part[c] = panel_product(own, own, c, rb, bs) + panel_product(inner, from_inner, c, rb, bs)
        outer_part[c] = panel_product(own, outer, c, rb, bs)

    drop_absent(s_inner, pattern, me, partner, rb, bs)
    drop_absent(s_from_inner, pattern, partner, me, rb, bs)


def square_kernel(
    devices, rb, bs, pattern, own, inner, outer, from_outer, s_inner, s_from_inner, own_part,
    s_own, s_head, s_tail, from_outer_part, cube_part, inner_part,
):
    me, _, _ = neighbours(devices)

    @pl.loop(0, rb)
    def _(c):
        s_own[c] = (own_part[c] + panel_product(outer, from_outer, c, rb, bs)).astype(BF16)

    drop_absent(s_own, pattern, me, me, rb, bs)
    s_head[...] = s_own[pl.ds(0, rb - 1)]
    s_tail[...] = s_own[pl.ds(rb - 1, 1)]

    @pl.loop(0, rb)
    def _(c):
        from_outer_part[c] = panel_product(from_outer, own, c, rb, bs)
        cube_part[c] = panel_product(own, s_own, c, rb, bs) + panel_product(inner, s_from_inner, c, rb, bs)
        inner_part[c] = 3.0 * s_inner[c].astype(F32) - 2.0 * panel_product(own, s_inner, c, rb, bs)


def late_kernel(
    devices, rb, bs, pattern, own, outer, inner, outer_own, from_outer, s_own, s_inner_own, outer_part,
    from_outer_part, cube_part, inner_part, out, rest, s_outer, s_from_outer, out_own, out_inner, sems,
):
    me, other, partner = neighbours(devices)
    waits = []
    for c in range(rb):
        out_inner[c] = (inner_part[c] - 2.0 * panel_product(inner, s_inner_own, c, rb, bs)).astype(BF16)
        waits += scatter(out, pattern, me, partner, out_inner, c, sems, 0, rb, bs)

    @pl.loop(0, rb)
    def _(c):
        s_from_outer[c] = (from_outer_part[c] + panel_product(outer_own, from_outer, c, rb, bs)).astype(BF16)
        s_outer[c] = (outer_part[c] + panel_product(outer, outer_own, c, rb, bs)).astype(BF16)

    drop_absent(s_outer, pattern, me, other, rb, bs)
    drop_absent(s_from_outer, pattern, other, me, rb, bs)
    for c in range(rb):
        cube = cube_part[c] + panel_product(outer, s_from_outer, c, rb, bs)
        out_own[c] = (3.0 * s_own[c].astype(F32) - 2.0 * cube).astype(BF16)
        waits += scatter(out, pattern, me, me, out_own, c, sems, rb * rb, rb, bs)

    @pl.loop(0, rb)
    def _(c):
        rest[c] = 3.0 * s_outer[c].astype(F32) - 2.0 * panel_product(own, s_outer, c, rb, bs)

    settle(waits)


def last_kernel(first, devices, rb, bs, pattern, outer, s_outer_own, rest, _, out, out_outer, sems):
    me, other, _ = neighbours(devices)
    waits = []
    for c in range(s_outer_own.shape[0]):
        cube = panel_product(outer, s_outer_own, c, rb, bs)
        out_outer[first + c] = (rest[first + c] - 2.0 * cube).astype(BF16)
        waits += scatter(out, pattern, me, other, out_outer, first + c, sems, 0, rb, bs)
    settle(waits)


def local(devices, block_values, pattern):
    rb, _, bs, _ = block_values.shape
    pattern = pattern.T
    over = [(i, (i + 1 if i % 2 else i - 1) % devices) for i in range(devices)]
    across = [(i, i ^ 1) for i in range(devices)]
    to_outer = lambda x: lax.ppermute(x, "grid", over)
    to_inner = lambda x: lax.ppermute(x, "grid", across)
    low_of = lambda panels: jax.ShapeDtypeStruct((panels, rb * bs, bs), BF16)
    low = low_of(rb)
    high = jax.ShapeDtypeStruct(low.shape, F32)
    full = jax.ShapeDtypeStruct(block_values.shape, BF16)

    def call(kernel, operands, outs, scratch=(), into=None):
        operands = (pltpu.with_memory_space_constraint(pattern, pltpu.SMEM), *operands)
        in_specs = [SMEM] + [VMEM] * (len(operands) - 1)
        aliases = {}
        if into is not None:
            aliases = {len(operands): 0}
            operands, in_specs = (*operands, into), in_specs + [ANY]
        scratch = [pltpu.VMEM(low.shape, BF16)] * scratch + [pltpu.SemaphoreType.DMA((2 * rb * rb,))] if scratch else []
        return pl.pallas_call(
            functools.partial(kernel, devices, rb, bs),
            out_shape=outs,
            in_specs=in_specs,
            out_specs=[ANY if out is full else VMEM for out in outs],
            scratch_shapes=scratch,
            input_output_aliases=aliases,
            compiler_params=pltpu.CompilerParams(vmem_limit_bytes=VMEM_LIMIT),
            cost_estimate=BRIEF,
            name=getattr(kernel, "func", kernel).__name__,
        )(*operands)

    outer, own, inner = pack(devices, pattern, block_values)
    from_outer = to_outer(outer)
    outer_own = to_outer(own)
    from_inner, inner_own = to_inner(inner), to_inner(own)

    s_inner, s_from_inner, own_part, outer_part = call(
        inner_kernel, (own, inner, outer, from_inner, inner_own), (low, low, high, high)
    )
    s_own, s_head, s_tail, from_outer_part, cube_part, inner_part = call(
        square_kernel,
        (own, inner, outer, from_outer, s_inner, s_from_inner, own_part),
        (low, low_of(rb - 1), low_of(1), high, high, high),
    )
    s_outer_head, s_outer_tail = to_outer(s_head), to_outer(s_tail)
    s_inner_own = to_inner(s_own)
    out, rest = call(
        late_kernel,
        (
            own, outer, inner, outer_own, from_outer, s_own, s_inner_own, outer_part, from_outer_part, cube_part,
            inner_part,
        ),
        (full, high),
        4,
    )
    (out,) = call(functools.partial(last_kernel, 0), (outer, s_outer_head, rest), (full,), 1, into=out)
    (out,) = call(functools.partial(last_kernel, rb - 1), (outer, s_outer_tail, rest), (full,), 1, into=out)
    return out


def solution(mesh):
    return jax.shard_map(
        functools.partial(local, mesh.shape["grid"]),
        mesh=mesh,
        in_specs=(P(("parts", "grid"), None, None, None), P("parts", None)),
        out_specs=P(("parts", "grid"), None, None, None),
        check_vma=False,
    )
```

```python
import functools

import jax
import jax.numpy as jnp
from jax import lax
from jax.experimental import pallas as pl
from jax.experimental.pallas import tpu as pltpu
from jax.sharding import PartitionSpec as P


F32 = jnp.float32
BF16 = jnp.bfloat16
ANY = pl.BlockSpec(memory_space=pl.ANY)
HBM = pl.BlockSpec(memory_space=pltpu.HBM)
VMEM = pl.BlockSpec(memory_space=pltpu.VMEM)
SMEM = pl.BlockSpec(memory_space=pltpu.SMEM)
BRIEF = pl.CostEstimate(flops=1, bytes_accessed=1, transcendentals=0)
VMEM_LIMIT = 24 * 1024 * 1024


def neighbours(devices):
    me = lax.axis_index("grid")
    odd = lax.rem(me, 2)
    above = lax.rem(me + 1, devices)
    below = lax.rem(me + devices - 1, devices)
    return me, jnp.where(odd == 1, above, below), jnp.where(odd == 1, below, above)


def slot_of(pattern, row, column):
    slot = jnp.int32(-1)
    for s in range(pattern.shape[0]):
        slot = jnp.where(pattern[s, row] == column, s, slot)
    return slot


def panel_product(left, right, c, rb, bs):
    total = jnp.dot(left[0], right[c, pl.ds(0, bs), :], preferred_element_type=F32)
    for k in range(1, rb):
        total += jnp.dot(left[k], right[c, pl.ds(k * bs, bs), :], preferred_element_type=F32)
    return total


def drop_absent(ref, pattern, row_device, column_device, rb, bs):
    for r in range(rb):
        for j in range(rb):
            slot = slot_of(pattern, row_device * rb + r, column_device * rb + j)

            @pl.when(slot < 0)
            def _():
                ref[j, pl.ds(r * bs, bs), :] = jnp.zeros((bs, bs), ref.dtype)


def pack_kernel(devices, rb, bs, pattern_hbm, blocks, *rest):
    cuts, (pattern, held, pattern_sem, sems) = rest[:3], rest[3:]
    fetch = pltpu.make_async_copy(pattern_hbm, pattern, pattern_sem)
    fetch.start()
    loads = [pltpu.make_async_copy(blocks.at[r], held.at[r], sems.at[r]) for r in range(rb)]
    for load in loads:
        load.start()
    me, other, partner = neighbours(devices)
    fetch.wait()
    slots = [
        [[slot_of(pattern, me * rb + r, column_device * rb + j) for j in range(rb)] for r in range(rb)]
        for column_device in (other, me, partner)
    ]
    for r in range(rb):
        loads[r].wait()
        for cut, rows in zip(cuts, slots):
            for j, slot in enumerate(rows[r]):
                block = held[r, jnp.maximum(slot, 0)]
                cut[j, pl.ds(r * bs, bs), :] = jnp.where(slot >= 0, block, jnp.zeros_like(block))


def pack(devices, pattern, blocks):
    rb, _, bs, _ = blocks.shape
    return pl.pallas_call(
        functools.partial(pack_kernel, devices, rb, bs),
        out_shape=[jax.ShapeDtypeStruct((rb, rb * bs, bs), blocks.dtype)] * 3,
        in_specs=[ANY, ANY],
        out_specs=[VMEM] * 3,
        scratch_shapes=[
            pltpu.SMEM(pattern.shape, pattern.dtype),
            pltpu.VMEM(blocks.shape, blocks.dtype),
            pltpu.SemaphoreType.DMA,
            pltpu.SemaphoreType.DMA((rb,)),
        ],
        compiler_params=pltpu.CompilerParams(vmem_limit_bytes=VMEM_LIMIT),
        cost_estimate=BRIEF,
        name="pack",
    )(
        pltpu.with_memory_space_constraint(pattern, pltpu.HBM),
        pltpu.with_memory_space_constraint(blocks, pltpu.HBM),
    )


def scatter(out, pattern, me, column_device, panels, j, sems, base, rb, bs):
    waits = []
    for r in range(rb):
        slot = slot_of(pattern, me * rb + r, column_device * rb + j)
        copy = pltpu.make_async_copy(
            panels.at[j, pl.ds(r * bs, bs), :], out.at[r, jnp.maximum(slot, 0)], sems.at[base + r * rb + j]
        )
        pl.when(slot >= 0)(copy.start)
        waits.append((slot, copy))
    return waits


def settle(waits):
    for slot, copy in waits:
        pl.when(slot >= 0)(copy.wait)


def outer_kernel(devices, rb, bs, pattern, outer, from_outer, own_part):
    @pl.loop(0, rb)
    def _(c):
        own_part[c] = panel_product(outer, from_outer, c, rb, bs)


def square_kernel(devices, rb, bs, pattern, own, inner, from_inner, own_part, s_own, s_head, s_tail):
    me, _, _ = neighbours(devices)

    @pl.loop(0, rb)
    def _(c):
        s_own[c] = (
            own_part[c] + panel_product(own, own, c, rb, bs) + panel_product(inner, from_inner, c, rb, bs)
        ).astype(BF16)

    drop_absent(s_own, pattern, me, me, rb, bs)
    s_head[...] = s_own[pl.ds(0, rb - 1)]
    s_tail[...] = s_own[pl.ds(rb - 1, 1)]


def early_kernel(
    devices, rb, bs, pattern, own, inner, outer, from_inner, inner_own, from_outer, s_own,
    cube_part, inner_part, from_outer_part, outer_part, s_inner, s_from_inner, sems,
):
    me, _, partner = neighbours(devices)

    @pl.loop(0, rb)
    def _(c):
        s_inner[c] = (panel_product(own, inner, c, rb, bs) + panel_product(inner, inner_own, c, rb, bs)).astype(BF16)
        s_from_inner[c] = (
            panel_product(from_inner, own, c, rb, bs) + panel_product(inner_own, from_inner, c, rb, bs)
        ).astype(BF16)
        from_outer_part[c] = panel_product(from_outer, own, c, rb, bs)
        outer_part[c] = panel_product(own, outer, c, rb, bs)

    drop_absent(s_inner, pattern, me, partner, rb, bs)
    drop_absent(s_from_inner, pattern, partner, me, rb, bs)

    @pl.loop(0, rb)
    def _(c):
        cube_part[c] = panel_product(own, s_own, c, rb, bs) + panel_product(inner, s_from_inner, c, rb, bs)
        inner_part[c] = 3.0 * s_inner[c].astype(F32) - 2.0 * panel_product(own, s_inner, c, rb, bs)


def late_kernel(
    devices, rb, bs, pattern, own, outer, outer_own, from_outer, s_own, outer_part, from_outer_part, cube_part,
    out, rest, s_outer, s_from_outer, out_own, sems,
):
    me, other, _ = neighbours(devices)

    @pl.loop(0, rb)
    def _(c):
        s_from_outer[c] = (from_outer_part[c] + panel_product(outer_own, from_outer, c, rb, bs)).astype(BF16)
        s_outer[c] = (outer_part[c] + panel_product(outer, outer_own, c, rb, bs)).astype(BF16)

    drop_absent(s_outer, pattern, me, other, rb, bs)
    drop_absent(s_from_outer, pattern, other, me, rb, bs)
    waits = []
    for c in range(rb):
        cube = cube_part[c] + panel_product(outer, s_from_outer, c, rb, bs)
        out_own[c] = (3.0 * s_own[c].astype(F32) - 2.0 * cube).astype(BF16)
        waits += scatter(out, pattern, me, me, out_own, c, sems, 0, rb, bs)

    @pl.loop(0, rb)
    def _(c):
        rest[c] = 3.0 * s_outer[c].astype(F32) - 2.0 * panel_product(own, s_outer, c, rb, bs)

    settle(waits)


def finish(devices, rb, bs, pattern, column_device, first, left, right, part, out, panels, sems, base):
    me = lax.axis_index("grid")
    waits = []
    for c in range(right.shape[0]):
        cube = panel_product(left, right, c, rb, bs)
        panels[first + c] = (part[first + c] - 2.0 * cube).astype(BF16)
        waits += scatter(out, pattern, me, column_device, panels, first + c, sems, base, rb, bs)
    return waits


def head_kernel(
    devices, rb, bs, pattern, outer, s_outer_head, rest, inner, s_inner_own, inner_part, _,
    out, out_outer, out_inner, sems,
):
    _, other, partner = neighbours(devices)
    waits = finish(devices, rb, bs, pattern, other, 0, outer, s_outer_head, rest, out, out_outer, sems, 0)
    waits += finish(
        devices, rb, bs, pattern, partner, 0, inner, s_inner_own, inner_part, out, out_inner, sems, rb * rb
    )
    settle(waits)


def tail_kernel(devices, rb, bs, pattern, outer, s_outer_tail, rest, _, out, out_outer, sems):
    _, other, _ = neighbours(devices)
    settle(finish(devices, rb, bs, pattern, other, rb - 1, outer, s_outer_tail, rest, out, out_outer, sems, 0))


def local(devices, block_values, pattern):
    rb, _, bs, _ = block_values.shape
    pattern = pattern.T
    over = [(i, (i + 1 if i % 2 else i - 1) % devices) for i in range(devices)]
    across = [(i, i ^ 1) for i in range(devices)]
    to_outer = lambda x: lax.ppermute(x, "grid", over)
    to_inner = lambda x: lax.ppermute(x, "grid", across)
    low_of = lambda panels: jax.ShapeDtypeStruct((panels, rb * bs, bs), BF16)
    low = low_of(rb)
    high = jax.ShapeDtypeStruct(low.shape, F32)
    full = jax.ShapeDtypeStruct(block_values.shape, BF16)

    def call(kernel, operands, outs, scratch=(), into=None):
        operands = (pltpu.with_memory_space_constraint(pattern, pltpu.SMEM), *operands)
        in_specs = [SMEM] + [VMEM] * (len(operands) - 1)
        aliases = {}
        if into is not None:
            aliases = {len(operands): 0}
            operands, in_specs = (*operands, into), in_specs + [ANY]
        scratch = [pltpu.VMEM(low.shape, BF16)] * scratch + [pltpu.SemaphoreType.DMA((2 * rb * rb,))] if scratch else []
        return pl.pallas_call(
            functools.partial(kernel, devices, rb, bs),
            out_shape=outs,
            in_specs=in_specs,
            out_specs=[ANY if out is full else VMEM for out in outs],
            scratch_shapes=scratch,
            input_output_aliases=aliases,
            compiler_params=pltpu.CompilerParams(vmem_limit_bytes=VMEM_LIMIT),
            cost_estimate=BRIEF,
            name=kernel.__name__,
        )(*operands)

    outer, own, inner = pack(devices, pattern, block_values)
    from_outer = to_outer(outer)
    outer_own = to_outer(own)
    from_inner, inner_own = to_inner(inner), to_inner(own)

    (own_part,) = call(outer_kernel, (outer, from_outer), (high,))
    s_own, s_head, s_tail = call(square_kernel, (own, inner, from_inner, own_part), (low, low_of(rb - 1), low_of(1)))
    s_outer_head, s_outer_tail = to_outer(s_head), to_outer(s_tail)
    s_inner_own = to_inner(s_own)
    cube_part, inner_part, from_outer_part, outer_part = call(
        early_kernel, (own, inner, outer, from_inner, inner_own, from_outer, s_own), (high,) * 4, 2
    )
    out, rest = call(
        late_kernel,
        (own, outer, outer_own, from_outer, s_own, outer_part, from_outer_part, cube_part),
        (full, high),
        3,
    )
    (out,) = call(
        head_kernel, (outer, s_outer_head, rest, inner, s_inner_own, inner_part), (full,), 2, into=out
    )
    (out,) = call(tail_kernel, (outer, s_outer_tail, rest), (full,), 1, into=out)
    return out


def solution(mesh):
    return jax.shard_map(
        functools.partial(local, mesh.shape["grid"]),
        mesh=mesh,
        in_specs=(P(("parts", "grid"), None, None, None), P("parts", None)),
        out_specs=P(("parts", "grid"), None, None, None),
        check_vma=False,
    )
```

```python
import functools

import jax
import jax.numpy as jnp
from jax import lax
from jax.experimental import pallas as pl
from jax.experimental.pallas import tpu as pltpu
from jax.sharding import PartitionSpec as P


F32 = jnp.float32
BF16 = jnp.bfloat16
ANY = pl.BlockSpec(memory_space=pl.ANY)
HBM = pl.BlockSpec(memory_space=pltpu.HBM)
VMEM = pl.BlockSpec(memory_space=pltpu.VMEM)
SMEM = pl.BlockSpec(memory_space=pltpu.SMEM)
BRIEF = pl.CostEstimate(flops=1, bytes_accessed=1, transcendentals=0)
VMEM_LIMIT = 24 * 1024 * 1024


def neighbours(devices):
    me = lax.axis_index("grid")
    odd = lax.rem(me, 2)
    above = lax.rem(me + 1, devices)
    below = lax.rem(me + devices - 1, devices)
    return me, jnp.where(odd == 1, above, below), jnp.where(odd == 1, below, above)


def slot_of(pattern, row, column):
    slot = jnp.int32(-1)
    for s in range(pattern.shape[0]):
        slot = jnp.where(pattern[s, row] == column, s, slot)
    return slot


def panel_product(left, right, c, rb, bs):
    total = jnp.dot(left[0], right[c, pl.ds(0, bs), :], preferred_element_type=F32)
    for k in range(1, rb):
        total += jnp.dot(left[k], right[c, pl.ds(k * bs, bs), :], preferred_element_type=F32)
    return total


def drop_absent(ref, pattern, row_device, column_device, rb, bs):
    for r in range(rb):
        for j in range(rb):
            slot = slot_of(pattern, row_device * rb + r, column_device * rb + j)

            @pl.when(slot < 0)
            def _():
                ref[j, pl.ds(r * bs, bs), :] = jnp.zeros((bs, bs), ref.dtype)


def pack_kernel(devices, rb, bs, pattern_hbm, blocks, *rest):
    cuts, (pattern, held, pattern_sem, sems) = rest[:3], rest[3:]
    fetch = pltpu.make_async_copy(pattern_hbm, pattern, pattern_sem)
    fetch.start()
    loads = [pltpu.make_async_copy(blocks.at[r], held.at[r], sems.at[r]) for r in range(rb)]
    for load in loads:
        load.start()
    me, other, partner = neighbours(devices)
    fetch.wait()
    slots = [
        [[slot_of(pattern, me * rb + r, column_device * rb + j) for j in range(rb)] for r in range(rb)]
        for column_device in (other, me, partner)
    ]
    for r in range(rb):
        loads[r].wait()
        for cut, rows in zip(cuts, slots):
            for j, slot in enumerate(rows[r]):
                block = held[r, jnp.maximum(slot, 0)]
                cut[j, pl.ds(r * bs, bs), :] = jnp.where(slot >= 0, block, jnp.zeros_like(block))


def pack(devices, pattern, blocks):
    rb, _, bs, _ = blocks.shape
    return pl.pallas_call(
        functools.partial(pack_kernel, devices, rb, bs),
        out_shape=[jax.ShapeDtypeStruct((rb, rb * bs, bs), blocks.dtype)] * 3,
        in_specs=[ANY, ANY],
        out_specs=[VMEM] * 3,
        scratch_shapes=[
            pltpu.SMEM(pattern.shape, pattern.dtype),
            pltpu.VMEM(blocks.shape, blocks.dtype),
            pltpu.SemaphoreType.DMA,
            pltpu.SemaphoreType.DMA((rb,)),
        ],
        compiler_params=pltpu.CompilerParams(vmem_limit_bytes=VMEM_LIMIT),
        cost_estimate=BRIEF,
        name="pack",
    )(
        pltpu.with_memory_space_constraint(pattern, pltpu.HBM),
        pltpu.with_memory_space_constraint(blocks, pltpu.HBM),
    )


def scatter(out, pattern, me, column_device, panels, j, sems, base, rb, bs):
    waits = []
    for r in range(rb):
        slot = slot_of(pattern, me * rb + r, column_device * rb + j)
        copy = pltpu.make_async_copy(
            panels.at[j, pl.ds(r * bs, bs), :], out.at[r, jnp.maximum(slot, 0)], sems.at[base + r * rb + j]
        )
        pl.when(slot >= 0)(copy.start)
        waits.append((slot, copy))
    return waits


def settle(waits):
    for slot, copy in waits:
        pl.when(slot >= 0)(copy.wait)


def outer_kernel(devices, rb, bs, pattern, outer, from_outer, own_part):
    @pl.loop(0, rb)
    def _(c):
        own_part[c] = panel_product(outer, from_outer, c, rb, bs)


def square_kernel(devices, rb, bs, pattern, own, inner, from_inner, own_part, s_own, s_head, s_tail):
    me, _, _ = neighbours(devices)

    @pl.loop(0, rb)
    def _(c):
        s_own[c] = (
            own_part[c] + panel_product(own, own, c, rb, bs) + panel_product(inner, from_inner, c, rb, bs)
        ).astype(BF16)

    drop_absent(s_own, pattern, me, me, rb, bs)
    s_head[...] = s_own[pl.ds(0, rb - 1)]
    s_tail[...] = s_own[pl.ds(rb - 1, 1)]


def early_kernel(
    devices, rb, bs, pattern, own, inner, outer, from_inner, inner_own, from_outer, s_own,
    cube_part, inner_part, from_outer_part, outer_part, s_inner, s_from_inner, sems,
):
    me, _, partner = neighbours(devices)

    @pl.loop(0, rb)
    def _(c):
        s_inner[c] = (panel_product(own, inner, c, rb, bs) + panel_product(inner, inner_own, c, rb, bs)).astype(BF16)
        s_from_inner[c] = (
            panel_product(from_inner, own, c, rb, bs) + panel_product(inner_own, from_inner, c, rb, bs)
        ).astype(BF16)
        from_outer_part[c] = panel_product(from_outer, own, c, rb, bs)
        outer_part[c] = panel_product(own, outer, c, rb, bs)

    drop_absent(s_inner, pattern, me, partner, rb, bs)
    drop_absent(s_from_inner, pattern, partner, me, rb, bs)

    @pl.loop(0, rb)
    def _(c):
        cube_part[c] = panel_product(own, s_own, c, rb, bs) + panel_product(inner, s_from_inner, c, rb, bs)
        inner_part[c] = 3.0 * s_inner[c].astype(F32) - 2.0 * panel_product(own, s_inner, c, rb, bs)


def late_kernel(
    devices, rb, bs, pattern, own, outer, outer_own, from_outer, s_own, outer_part, from_outer_part, cube_part,
    out, rest, slots, s_outer, s_from_outer, out_own, sems,
):
    me, other, _ = neighbours(devices)
    for r in range(rb):
        slots[r] = jnp.full(slots.shape[1:], slot_of(pattern, me * rb + r, other * rb + rb - 1))

    @pl.loop(0, rb)
    def _(c):
        s_from_outer[c] = (from_outer_part[c] + panel_product(outer_own, from_outer, c, rb, bs)).astype(BF16)
        s_outer[c] = (outer_part[c] + panel_product(outer, outer_own, c, rb, bs)).astype(BF16)

    drop_absent(s_outer, pattern, me, other, rb, bs)
    drop_absent(s_from_outer, pattern, other, me, rb, bs)
    waits = []
    for c in range(rb):
        cube = cube_part[c] + panel_product(outer, s_from_outer, c, rb, bs)
        out_own[c] = (3.0 * s_own[c].astype(F32) - 2.0 * cube).astype(BF16)
        waits += scatter(out, pattern, me, me, out_own, c, sems, 0, rb, bs)

    @pl.loop(0, rb)
    def _(c):
        rest[c] = 3.0 * s_outer[c].astype(F32) - 2.0 * panel_product(own, s_outer, c, rb, bs)

    settle(waits)


def finish(devices, rb, bs, pattern, column_device, first, left, right, part, out, panels, sems, base):
    me = lax.axis_index("grid")
    waits = []
    for c in range(right.shape[0]):
        cube = panel_product(left, right, c, rb, bs)
        panels[first + c] = (part[first + c] - 2.0 * cube).astype(BF16)
        waits += scatter(out, pattern, me, column_device, panels, first + c, sems, base, rb, bs)
    return waits


def head_kernel(
    devices, rb, bs, pattern, outer, s_outer_head, rest, inner, s_inner_own, inner_part, _,
    out, out_outer, out_inner, sems,
):
    _, other, partner = neighbours(devices)
    waits = finish(devices, rb, bs, pattern, other, 0, outer, s_outer_head, rest, out, out_outer, sems, 0)
    waits += finish(
        devices, rb, bs, pattern, partner, 0, inner, s_inner_own, inner_part, out, out_inner, sems, rb * rb
    )
    settle(waits)


def tail_kernel(devices, rb, bs, slots, outer, s_outer_tail, rest, _, out, panels, sems):
    waits = []
    for r in range(rb):
        rows = pl.ds(r * bs, bs)
        slot = jnp.max(slots[r])
        cube = jnp.dot(outer[0, rows, :], s_outer_tail[0, pl.ds(0, bs), :], preferred_element_type=F32)
        for k in range(1, rb):
            cube += jnp.dot(outer[k, rows, :], s_outer_tail[0, pl.ds(k * bs, bs), :], preferred_element_type=F32)
        panels[0, rows, :] = (rest[rb - 1, rows, :] - 2.0 * cube).astype(BF16)
        copy = pltpu.make_async_copy(panels.at[0, rows, :], out.at[r, jnp.maximum(slot, 0)], sems.at[r])
        pl.when(slot >= 0)(copy.start)
        waits.append((slot, copy))
    settle(waits)


def local(devices, block_values, pattern):
    rb, _, bs, _ = block_values.shape
    pattern = pattern.T
    over = [(i, (i + 1 if i % 2 else i - 1) % devices) for i in range(devices)]
    across = [(i, i ^ 1) for i in range(devices)]
    to_outer = lambda x: lax.ppermute(x, "grid", over)
    to_inner = lambda x: lax.ppermute(x, "grid", across)
    low_of = lambda panels: jax.ShapeDtypeStruct((panels, rb * bs, bs), BF16)
    low = low_of(rb)
    high = jax.ShapeDtypeStruct(low.shape, F32)
    full = jax.ShapeDtypeStruct(block_values.shape, BF16)

    def call(kernel, operands, outs, scratch=(), into=None):
        operands = (pltpu.with_memory_space_constraint(pattern, pltpu.SMEM), *operands)
        in_specs = [SMEM] + [VMEM] * (len(operands) - 1)
        aliases = {}
        if into is not None:
            aliases = {len(operands): 0}
            operands, in_specs = (*operands, into), in_specs + [ANY]
        scratch = [pltpu.VMEM(low.shape, BF16)] * scratch + [pltpu.SemaphoreType.DMA((2 * rb * rb,))] if scratch else []
        return pl.pallas_call(
            functools.partial(kernel, devices, rb, bs),
            out_shape=outs,
            in_specs=in_specs,
            out_specs=[ANY if out is full else VMEM for out in outs],
            scratch_shapes=scratch,
            input_output_aliases=aliases,
            compiler_params=pltpu.CompilerParams(vmem_limit_bytes=VMEM_LIMIT),
            cost_estimate=BRIEF,
            name=kernel.__name__,
        )(*operands)

    outer, own, inner = pack(devices, pattern, block_values)
    from_outer = to_outer(outer)
    outer_own = to_outer(own)
    from_inner, inner_own = to_inner(inner), to_inner(own)

    (own_part,) = call(outer_kernel, (outer, from_outer), (high,))
    s_own, s_head, s_tail = call(square_kernel, (own, inner, from_inner, own_part), (low, low_of(rb - 1), low_of(1)))
    s_outer_head, s_outer_tail = to_outer(s_head), to_outer(s_tail)
    s_inner_own = to_inner(s_own)
    cube_part, inner_part, from_outer_part, outer_part = call(
        early_kernel, (own, inner, outer, from_inner, inner_own, from_outer, s_own), (high,) * 4, 2
    )
    out, rest, slots = call(
        late_kernel,
        (own, outer, outer_own, from_outer, s_own, outer_part, from_outer_part, cube_part),
        (full, high, jax.ShapeDtypeStruct((rb, 8, 128), jnp.int32)),
        3,
    )
    (out,) = call(
        head_kernel, (outer, s_outer_head, rest, inner, s_inner_own, inner_part), (full,), 2, into=out
    )
    return pl.pallas_call(
        functools.partial(tail_kernel, devices, rb, bs),
        out_shape=full,
        in_specs=[VMEM, VMEM, VMEM, VMEM, ANY],
        out_specs=ANY,
        scratch_shapes=[pltpu.VMEM((1, rb * bs, bs), BF16), pltpu.SemaphoreType.DMA((rb,))],
        input_output_aliases={4: 0},
        compiler_params=pltpu.CompilerParams(vmem_limit_bytes=VMEM_LIMIT),
        cost_estimate=BRIEF,
        name="tail_kernel",
    )(slots, outer, s_outer_tail, rest, out)


def solution(mesh):
    return jax.shard_map(
        functools.partial(local, mesh.shape["grid"]),
        mesh=mesh,
        in_specs=(P(("parts", "grid"), None, None, None), P("parts", None)),
        out_specs=P(("parts", "grid"), None, None, None),
        check_vma=False,
    )
```

```python
import functools

import jax
import jax.numpy as jnp
from jax import lax
from jax.experimental import pallas as pl
from jax.experimental.pallas import tpu as pltpu
from jax.sharding import PartitionSpec as P


F32 = jnp.float32
BF16 = jnp.bfloat16
ANY = pl.BlockSpec(memory_space=pl.ANY)
HBM = pl.BlockSpec(memory_space=pltpu.HBM)
VMEM = pl.BlockSpec(memory_space=pltpu.VMEM)
SMEM = pl.BlockSpec(memory_space=pltpu.SMEM)
BRIEF = pl.CostEstimate(flops=1, bytes_accessed=1, transcendentals=0)
LONGER = pl.CostEstimate(flops=5 * 10**9, bytes_accessed=1, transcendentals=0)
VMEM_LIMIT = 24 * 1024 * 1024


def neighbours(devices):
    me = lax.axis_index("grid")
    odd = lax.rem(me, 2)
    above = lax.rem(me + 1, devices)
    below = lax.rem(me + devices - 1, devices)
    return me, jnp.where(odd == 1, above, below), jnp.where(odd == 1, below, above)


def slot_of(pattern, row, column):
    slot = jnp.int32(-1)
    for s in range(pattern.shape[0]):
        slot = jnp.where(pattern[s, row] == column, s, slot)
    return slot


def panel_product(left, right, c, rb, bs):
    total = jnp.dot(left[0], right[c, pl.ds(0, bs), :], preferred_element_type=F32)
    for k in range(1, rb):
        total += jnp.dot(left[k], right[c, pl.ds(k * bs, bs), :], preferred_element_type=F32)
    return total


def drop_absent(ref, pattern, row_device, column_device, rb, bs):
    for r in range(rb):
        for j in range(rb):
            slot = slot_of(pattern, row_device * rb + r, column_device * rb + j)

            @pl.when(slot < 0)
            def _():
                ref[j, pl.ds(r * bs, bs), :] = jnp.zeros((bs, bs), ref.dtype)


def place(pattern, held, row, owner, columns, cut, first, rb, bs):
    for j in range(rb):
        slot = slot_of(pattern, owner * rb + row, columns * rb + j)
        block = held[jnp.maximum(slot, 0)]
        cut[j, pl.ds((row - first) * bs, bs), :] = jnp.where(slot >= 0, block, jnp.zeros_like(block))


def first_kernel(devices, rb, bs, pattern_hbm, blocks, cut, pattern, held, pattern_sem, sem):
    fetch = pltpu.make_async_copy(pattern_hbm, pattern, pattern_sem)
    fetch.start()
    load = pltpu.make_async_copy(blocks.at[0], held, sem)
    load.start()
    me, other, _ = neighbours(devices)
    fetch.wait()
    load.wait()
    place(pattern, held, 0, me, other, cut, 0, rb, bs)


def pack_kernel(devices, rb, bs, pattern_hbm, blocks, _, others, *rest):
    cuts, (pattern, held, pattern_sem, sems) = rest[:3], rest[3:]
    fetch = pltpu.make_async_copy(pattern_hbm, pattern, pattern_sem)
    fetch.start()
    loads = [pltpu.make_async_copy(blocks.at[r], held.at[r], sems.at[r]) for r in range(rb)]
    for load in loads:
        load.start()
    people = neighbours(devices)
    me, other, partner = people
    fetch.wait()
    for r in range(rb):
        loads[r].wait()
        for cut, columns in zip(cuts, (other, me, partner)):
            place(pattern, held.at[r], r, me, columns, cut, 0, rb, bs)
    others[...] = cuts[0][:, pl.ds(bs, (rb - 1) * bs), :]


def pack(devices, pattern, blocks):
    rb, slots, bs, _ = blocks.shape
    pattern = pltpu.with_memory_space_constraint(pattern, pltpu.HBM)
    blocks = pltpu.with_memory_space_constraint(blocks, pltpu.HBM)
    cut = lambda rows: jax.ShapeDtypeStruct((rb, rows * bs, bs), blocks.dtype)
    params = pltpu.CompilerParams(vmem_limit_bytes=VMEM_LIMIT)
    first = pl.pallas_call(
        functools.partial(first_kernel, devices, rb, bs),
        out_shape=cut(1),
        in_specs=[ANY, ANY],
        out_specs=VMEM,
        scratch_shapes=[
            pltpu.SMEM(pattern.shape, pattern.dtype),
            pltpu.VMEM(blocks.shape[1:], blocks.dtype),
            pltpu.SemaphoreType.DMA,
            pltpu.SemaphoreType.DMA,
        ],
        compiler_params=params,
        cost_estimate=BRIEF,
        name="first",
    )(pattern, blocks)
    return first, *pl.pallas_call(
        functools.partial(pack_kernel, devices, rb, bs),
        out_shape=[cut(rb - 1), cut(rb), cut(rb), cut(rb)],
        in_specs=[ANY, ANY, ANY],
        out_specs=[VMEM] * 4,
        scratch_shapes=[
            pltpu.SMEM(pattern.shape, pattern.dtype),
            pltpu.VMEM(blocks.shape, blocks.dtype),
            pltpu.SemaphoreType.DMA,
            pltpu.SemaphoreType.DMA((rb,)),
        ],
        compiler_params=params,
        cost_estimate=BRIEF,
        name="pack",
    )(pattern, blocks, first)


def scatter(out, pattern, me, column_device, panels, j, sems, base, rb, bs):
    waits = []
    for r in range(rb):
        slot = slot_of(pattern, me * rb + r, column_device * rb + j)
        copy = pltpu.make_async_copy(
            panels.at[j, pl.ds(r * bs, bs), :], out.at[r, jnp.maximum(slot, 0)], sems.at[base + r * rb + j]
        )
        pl.when(slot >= 0)(copy.start)
        waits.append((slot, copy))
    return waits


def settle(waits):
    for slot, copy in waits:
        pl.when(slot >= 0)(copy.wait)


def begin_kernel(devices, rb, bs, outer, from_first, part):
    @pl.loop(0, rb)
    def _(c):
        part[c] = jnp.dot(outer[0], from_first[c], preferred_element_type=F32)


def outer_kernel(devices, rb, bs, outer, from_first, from_others, part, from_outer, own_part):
    from_outer[:, pl.ds(0, bs), :] = from_first[...]
    from_outer[:, pl.ds(bs, (rb - 1) * bs), :] = from_others[...]

    @pl.loop(0, rb)
    def _(c):
        total = part[c]
        for k in range(1, rb):
            total += jnp.dot(outer[k], from_others[c, pl.ds((k - 1) * bs, bs), :], preferred_element_type=F32)
        own_part[c] = total


def square_kernel(devices, rb, bs, pattern, own, inner, from_inner, own_part, s_own, s_head, s_tail):
    me, _, _ = neighbours(devices)

    @pl.loop(0, rb)
    def _(c):
        s_own[c] = (
            own_part[c] + panel_product(own, own, c, rb, bs) + panel_product(inner, from_inner, c, rb, bs)
        ).astype(BF16)

    drop_absent(s_own, pattern, me, me, rb, bs)
    s_head[...] = s_own[pl.ds(0, rb - 1)]
    s_tail[...] = s_own[pl.ds(rb - 1, 1)]


def early_kernel(
    devices, rb, bs, pattern, own, inner, outer, from_inner, inner_own, from_outer, s_own,
    cube_part, inner_part, from_outer_part, outer_part, s_inner, s_from_inner, sems,
):
    me, _, partner = neighbours(devices)

    @pl.loop(0, rb)
    def _(c):
        s_inner[c] = (panel_product(own, inner, c, rb, bs) + panel_product(inner, inner_own, c, rb, bs)).astype(BF16)
        s_from_inner[c] = (
            panel_product(from_inner, own, c, rb, bs) + panel_product(inner_own, from_inner, c, rb, bs)
        ).astype(BF16)
        from_outer_part[c] = panel_product(from_outer, own, c, rb, bs)
        outer_part[c] = panel_product(own, outer, c, rb, bs)

    drop_absent(s_inner, pattern, me, partner, rb, bs)
    drop_absent(s_from_inner, pattern, partner, me, rb, bs)

    @pl.loop(0, rb)
    def _(c):
        cube_part[c] = panel_product(own, s_own, c, rb, bs) + panel_product(inner, s_from_inner, c, rb, bs)
        inner_part[c] = 3.0 * s_inner[c].astype(F32) - 2.0 * panel_product(own, s_inner, c, rb, bs)


def late_kernel(
    devices, rb, bs, pattern, own, outer, outer_own, from_outer, s_own, outer_part, from_outer_part, cube_part,
    out, rest, slots, s_outer, s_from_outer, out_own, sems,
):
    me, other, _ = neighbours(devices)
    for r in range(rb):
        slots[r] = jnp.full(slots.shape[1:], slot_of(pattern, me * rb + r, other * rb + rb - 1))

    @pl.loop(0, rb)
    def _(c):
        s_from_outer[c] = (from_outer_part[c] + panel_product(outer_own, from_outer, c, rb, bs)).astype(BF16)
        s_outer[c] = (outer_part[c] + panel_product(outer, outer_own, c, rb, bs)).astype(BF16)

    drop_absent(s_outer, pattern, me, other, rb, bs)
    drop_absent(s_from_outer, pattern, other, me, rb, bs)
    waits = []
    for c in range(rb):
        cube = cube_part[c] + panel_product(outer, s_from_outer, c, rb, bs)
        out_own[c] = (3.0 * s_own[c].astype(F32) - 2.0 * cube).astype(BF16)
        waits += scatter(out, pattern, me, me, out_own, c, sems, 0, rb, bs)

    @pl.loop(0, rb)
    def _(c):
        rest[c] = 3.0 * s_outer[c].astype(F32) - 2.0 * panel_product(own, s_outer, c, rb, bs)

    settle(waits)


def finish(devices, rb, bs, pattern, column_device, first, left, right, part, out, panels, sems, base):
    me = lax.axis_index("grid")
    waits = []
    for c in range(right.shape[0]):
        cube = panel_product(left, right, c, rb, bs)
        panels[first + c] = (part[first + c] - 2.0 * cube).astype(BF16)
        waits += scatter(out, pattern, me, column_device, panels, first + c, sems, base, rb, bs)
    return waits


def head_kernel(
    devices, rb, bs, pattern, outer, s_outer_head, rest, inner, s_inner_own, inner_part, _,
    out, out_outer, out_inner, sems,
):
    _, other, partner = neighbours(devices)
    waits = finish(devices, rb, bs, pattern, other, 0, outer, s_outer_head, rest, out, out_outer, sems, 0)
    waits += finish(
        devices, rb, bs, pattern, partner, 0, inner, s_inner_own, inner_part, out, out_inner, sems, rb * rb
    )
    settle(waits)


def tail_kernel(devices, rb, bs, slots, outer, s_outer_tail, rest, _, out, panels, sems):
    waits = []
    for r in range(rb):
        rows = pl.ds(r * bs, bs)
        slot = jnp.max(slots[r])
        cube = jnp.dot(outer[0, rows, :], s_outer_tail[0, pl.ds(0, bs), :], preferred_element_type=F32)
        for k in range(1, rb):
            cube += jnp.dot(outer[k, rows, :], s_outer_tail[0, pl.ds(k * bs, bs), :], preferred_element_type=F32)
        panels[0, rows, :] = (rest[rb - 1, rows, :] - 2.0 * cube).astype(BF16)
        copy = pltpu.make_async_copy(panels.at[0, rows, :], out.at[r, jnp.maximum(slot, 0)], sems.at[r])
        pl.when(slot >= 0)(copy.start)
        waits.append((slot, copy))
    settle(waits)


def local(devices, block_values, pattern):
    rb, _, bs, _ = block_values.shape
    pattern = pattern.T
    over = [(i, (i + 1 if i % 2 else i - 1) % devices) for i in range(devices)]
    across = [(i, i ^ 1) for i in range(devices)]
    to_outer = lambda x: lax.ppermute(x, "grid", over)
    to_inner = lambda x: lax.ppermute(x, "grid", across)
    low_of = lambda panels: jax.ShapeDtypeStruct((panels, rb * bs, bs), BF16)
    low = low_of(rb)
    high = jax.ShapeDtypeStruct(low.shape, F32)
    full = jax.ShapeDtypeStruct(block_values.shape, BF16)

    def call(kernel, operands, outs, scratch=(), into=None, patterned=True, cost=BRIEF):
        in_specs = [VMEM] * len(operands)
        if patterned:
            operands = (pltpu.with_memory_space_constraint(pattern, pltpu.SMEM), *operands)
            in_specs = [SMEM] + in_specs
        aliases = {}
        if into is not None:
            aliases = {len(operands): 0}
            operands, in_specs = (*operands, into), in_specs + [ANY]
        scratch = [pltpu.VMEM(low.shape, BF16)] * scratch + [pltpu.SemaphoreType.DMA((2 * rb * rb,))] if scratch else []
        return pl.pallas_call(
            functools.partial(kernel, devices, rb, bs),
            out_shape=outs,
            in_specs=in_specs,
            out_specs=[ANY if out is full else VMEM for out in outs],
            scratch_shapes=scratch,
            input_output_aliases=aliases,
            compiler_params=pltpu.CompilerParams(vmem_limit_bytes=VMEM_LIMIT),
            cost_estimate=cost,
            name=kernel.__name__,
        )(*operands)

    first, others, outer, own, inner = pack(devices, pattern, block_values)
    from_first, from_others = to_outer(first), to_outer(others)
    outer_own = to_outer(own)
    from_inner, inner_own = to_inner(inner), to_inner(own)

    (part,) = call(begin_kernel, (outer, from_first), (high,), patterned=False, cost=LONGER)
    from_outer, own_part = call(outer_kernel, (outer, from_first, from_others, part), (low, high), patterned=False, cost=LONGER)
    s_own, s_head, s_tail = call(square_kernel, (own, inner, from_inner, own_part), (low, low_of(rb - 1), low_of(1)))
    s_outer_head, s_outer_tail = to_outer(s_head), to_outer(s_tail)
    s_inner_own = to_inner(s_own)
    cube_part, inner_part, from_outer_part, outer_part = call(
        early_kernel, (own, inner, outer, from_inner, inner_own, from_outer, s_own), (high,) * 4, 2
    )
    out, rest, slots = call(
        late_kernel,
        (own, outer, outer_own, from_outer, s_own, outer_part, from_outer_part, cube_part),
        (full, high, jax.ShapeDtypeStruct((rb, 8, 128), jnp.int32)),
        3,
    )
    (out,) = call(
        head_kernel, (outer, s_outer_head, rest, inner, s_inner_own, inner_part), (full,), 2, into=out
    )
    return pl.pallas_call(
        functools.partial(tail_kernel, devices, rb, bs),
        out_shape=full,
        in_specs=[VMEM, VMEM, VMEM, VMEM, ANY],
        out_specs=ANY,
        scratch_shapes=[pltpu.VMEM((1, rb * bs, bs), BF16), pltpu.SemaphoreType.DMA((rb,))],
        input_output_aliases={4: 0},
        compiler_params=pltpu.CompilerParams(vmem_limit_bytes=VMEM_LIMIT),
        cost_estimate=BRIEF,
        name="tail_kernel",
    )(slots, outer, s_outer_tail, rest, out)


def solution(mesh):
    return jax.shard_map(
        functools.partial(local, mesh.shape["grid"]),
        mesh=mesh,
        in_specs=(P(("parts", "grid"), None, None, None), P("parts", None)),
        out_specs=P(("parts", "grid"), None, None, None),
        check_vma=False,
    )
```

```python
import functools

import jax
import jax.numpy as jnp
from jax import lax
from jax.experimental import pallas as pl
from jax.experimental.pallas import tpu as pltpu
from jax.sharding import PartitionSpec as P


F32 = jnp.float32
BF16 = jnp.bfloat16
ANY = pl.BlockSpec(memory_space=pl.ANY)
HBM = pl.BlockSpec(memory_space=pltpu.HBM)
VMEM = pl.BlockSpec(memory_space=pltpu.VMEM)
SMEM = pl.BlockSpec(memory_space=pltpu.SMEM)
BRIEF = pl.CostEstimate(flops=1, bytes_accessed=1, transcendentals=0)
LONGER = pl.CostEstimate(flops=5 * 10**9, bytes_accessed=1, transcendentals=0)
VMEM_LIMIT = 24 * 1024 * 1024


def neighbours(devices):
    me = lax.axis_index("grid")
    odd = lax.rem(me, 2)
    above = lax.rem(me + 1, devices)
    below = lax.rem(me + devices - 1, devices)
    return me, jnp.where(odd == 1, above, below), jnp.where(odd == 1, below, above)


def slot_of(pattern, row, column):
    slot = jnp.int32(-1)
    for s in range(pattern.shape[0]):
        slot = jnp.where(pattern[s, row] == column, s, slot)
    return slot


def panel_product(left, right, c, rb, bs):
    total = jnp.dot(left[0], right[c, pl.ds(0, bs), :], preferred_element_type=F32)
    for k in range(1, rb):
        total += jnp.dot(left[k], right[c, pl.ds(k * bs, bs), :], preferred_element_type=F32)
    return total


def drop_absent(ref, pattern, row_device, column_device, rb, bs, panels=None):
    for r in range(rb):
        for j in range(rb if panels is None else panels):
            slot = slot_of(pattern, row_device * rb + r, column_device * rb + j)

            @pl.when(slot < 0)
            def _():
                ref[j, pl.ds(r * bs, bs), :] = jnp.zeros((bs, bs), ref.dtype)


def place(pattern, held, row, owner, columns, cut, first, rb, bs):
    for j in range(rb):
        slot = slot_of(pattern, owner * rb + row, columns * rb + j)
        block = held[jnp.maximum(slot, 0)]
        cut[j, pl.ds((row - first) * bs, bs), :] = jnp.where(slot >= 0, block, jnp.zeros_like(block))


def first_kernel(devices, rb, bs, pattern_hbm, blocks, cut, pattern, held, pattern_sem, sem):
    fetch = pltpu.make_async_copy(pattern_hbm, pattern, pattern_sem)
    fetch.start()
    load = pltpu.make_async_copy(blocks.at[0], held, sem)
    load.start()
    me, other, _ = neighbours(devices)
    fetch.wait()
    load.wait()
    place(pattern, held, 0, me, other, cut, 0, rb, bs)


def pack_kernel(devices, rb, bs, pattern_hbm, blocks, _, others, *rest):
    cuts, (pattern, held, pattern_sem, sems) = rest[:3], rest[3:]
    fetch = pltpu.make_async_copy(pattern_hbm, pattern, pattern_sem)
    fetch.start()
    loads = [pltpu.make_async_copy(blocks.at[r], held.at[r], sems.at[r]) for r in range(rb)]
    for load in loads:
        load.start()
    people = neighbours(devices)
    me, other, partner = people
    fetch.wait()
    for r in range(rb):
        loads[r].wait()
        for cut, columns in zip(cuts, (other, me, partner)):
            place(pattern, held.at[r], r, me, columns, cut, 0, rb, bs)
    others[...] = cuts[0][:, pl.ds(bs, (rb - 1) * bs), :]


def pack(devices, pattern, blocks):
    rb, slots, bs, _ = blocks.shape
    pattern = pltpu.with_memory_space_constraint(pattern, pltpu.HBM)
    blocks = pltpu.with_memory_space_constraint(blocks, pltpu.HBM)
    cut = lambda rows: jax.ShapeDtypeStruct((rb, rows * bs, bs), blocks.dtype)
    params = pltpu.CompilerParams(vmem_limit_bytes=VMEM_LIMIT)
    first = pl.pallas_call(
        functools.partial(first_kernel, devices, rb, bs),
        out_shape=cut(1),
        in_specs=[ANY, ANY],
        out_specs=VMEM,
        scratch_shapes=[
            pltpu.SMEM(pattern.shape, pattern.dtype),
            pltpu.VMEM(blocks.shape[1:], blocks.dtype),
            pltpu.SemaphoreType.DMA,
            pltpu.SemaphoreType.DMA,
        ],
        compiler_params=params,
        cost_estimate=BRIEF,
        name="first",
    )(pattern, blocks)
    return first, *pl.pallas_call(
        functools.partial(pack_kernel, devices, rb, bs),
        out_shape=[cut(rb - 1), cut(rb), cut(rb), cut(rb)],
        in_specs=[ANY, ANY, ANY],
        out_specs=[VMEM] * 4,
        scratch_shapes=[
            pltpu.SMEM(pattern.shape, pattern.dtype),
            pltpu.VMEM(blocks.shape, blocks.dtype),
            pltpu.SemaphoreType.DMA,
            pltpu.SemaphoreType.DMA((rb,)),
        ],
        compiler_params=params,
        cost_estimate=BRIEF,
        name="pack",
    )(pattern, blocks, first)


def scatter(out, pattern, me, column_device, panels, j, sems, base, rb, bs):
    waits = []
    for r in range(rb):
        slot = slot_of(pattern, me * rb + r, column_device * rb + j)
        copy = pltpu.make_async_copy(
            panels.at[j, pl.ds(r * bs, bs), :], out.at[r, jnp.maximum(slot, 0)], sems.at[base + r * rb + j]
        )
        pl.when(slot >= 0)(copy.start)
        waits.append((slot, copy))
    return waits


def settle(waits):
    for slot, copy in waits:
        pl.when(slot >= 0)(copy.wait)


def begin_kernel(devices, rb, bs, outer, from_first, part):
    @pl.loop(0, rb)
    def _(c):
        part[c] = jnp.dot(outer[0], from_first[c], preferred_element_type=F32)


def outer_kernel(devices, rb, bs, outer, from_first, from_others, part, from_outer, own_part):
    from_outer[:, pl.ds(0, bs), :] = from_first[...]
    from_outer[:, pl.ds(bs, (rb - 1) * bs), :] = from_others[...]

    @pl.loop(0, rb)
    def _(c):
        total = part[c]
        for k in range(1, rb):
            total += jnp.dot(outer[k], from_others[c, pl.ds((k - 1) * bs, bs), :], preferred_element_type=F32)
        own_part[c] = total


def square_kernel(devices, rb, bs, pattern, own, inner, from_inner, own_part, s_own, s_head):
    me, _, _ = neighbours(devices)

    @pl.loop(0, rb)
    def _(c):
        s_own[c] = (
            own_part[c] + panel_product(own, own, c, rb, bs) + panel_product(inner, from_inner, c, rb, bs)
        ).astype(BF16)

    drop_absent(s_own, pattern, me, me, rb, bs)
    s_head[...] = s_own[pl.ds(0, rb - 1)]


def early_kernel(
    devices, rb, bs, pattern, own, inner, outer, from_inner, inner_own, from_outer, s_own,
    cube_part, inner_part, from_outer_part, outer_part, s_inner, s_from_inner, sems,
):
    me, _, partner = neighbours(devices)

    @pl.loop(0, rb)
    def _(c):
        s_inner[c] = (panel_product(own, inner, c, rb, bs) + panel_product(inner, inner_own, c, rb, bs)).astype(BF16)
        s_from_inner[c] = (
            panel_product(from_inner, own, c, rb, bs) + panel_product(inner_own, from_inner, c, rb, bs)
        ).astype(BF16)
        from_outer_part[c] = panel_product(from_outer, own, c, rb, bs)
        outer_part[c] = panel_product(own, outer, c, rb, bs)

    drop_absent(s_inner, pattern, me, partner, rb, bs)
    drop_absent(s_from_inner, pattern, partner, me, rb, bs)

    @pl.loop(0, rb)
    def _(c):
        cube_part[c] = panel_product(own, s_own, c, rb, bs) + panel_product(inner, s_from_inner, c, rb, bs)
        inner_part[c] = 3.0 * s_inner[c].astype(F32) - 2.0 * panel_product(own, s_inner, c, rb, bs)


def ahead_kernel(
    devices, rb, bs, pattern, outer_own, from_outer, from_outer_part, s_own, s_from_outer, out_there, slots
):
    me, other, _ = neighbours(devices)
    last = rb - 1
    for r in range(rb):
        slots[r] = jnp.full(slots.shape[1:], slot_of(pattern, me * rb + r, other * rb + last))

    @pl.loop(0, rb)
    def _(c):
        s_from_outer[c] = (from_outer_part[c] + panel_product(outer_own, from_outer, c, rb, bs)).astype(BF16)

    drop_absent(s_from_outer, pattern, other, me, rb, bs)
    cube = panel_product(outer_own, s_from_outer, last, rb, bs) + panel_product(from_outer, s_own, last, rb, bs)
    out_there[0] = (3.0 * s_from_outer[last].astype(F32) - 2.0 * cube).astype(BF16)


def late_kernel(
    devices, rb, bs, pattern, own, outer, outer_own, s_from_outer, s_own, outer_part, cube_part, inner,
    s_inner_own, inner_part, out, rest, s_outer, out_own, out_inner, sems,
):
    me, other, partner = neighbours(devices)
    waits = []
    for c in range(rb):
        out_inner[c] = (inner_part[c] - 2.0 * panel_product(inner, s_inner_own, c, rb, bs)).astype(BF16)
        waits += scatter(out, pattern, me, partner, out_inner, c, sems, rb * rb, rb, bs)
    for c in range(rb):
        cube = cube_part[c] + panel_product(outer, s_from_outer, c, rb, bs)
        out_own[c] = (3.0 * s_own[c].astype(F32) - 2.0 * cube).astype(BF16)
        waits += scatter(out, pattern, me, me, out_own, c, sems, 0, rb, bs)

    @pl.loop(0, rb - 1)
    def _(c):
        s_outer[c] = (outer_part[c] + panel_product(outer, outer_own, c, rb, bs)).astype(BF16)

    drop_absent(s_outer, pattern, me, other, rb, bs, rb - 1)

    @pl.loop(0, rb - 1)
    def _(c):
        rest[c] = 3.0 * s_outer[c].astype(F32) - 2.0 * panel_product(own, s_outer, c, rb, bs)

    settle(waits)


def head_kernel(devices, rb, bs, pattern, outer, s_outer_head, rest, _, out, out_outer, sems):
    me, other, _ = neighbours(devices)
    waits = []
    for c in range(rb - 1):
        out_outer[c] = (rest[c] - 2.0 * panel_product(outer, s_outer_head, c, rb, bs)).astype(BF16)
        waits += scatter(out, pattern, me, other, out_outer, c, sems, 0, rb, bs)
    settle(waits)


def tail_kernel(rb, bs, slots, panel, _, out, sems):
    waits = []
    for r in range(rb):
        slot = jnp.max(slots[r])
        copy = pltpu.make_async_copy(panel.at[0, pl.ds(r * bs, bs), :], out.at[r, jnp.maximum(slot, 0)], sems.at[r])
        pl.when(slot >= 0)(copy.start)
        waits.append((slot, copy))
    settle(waits)


def local(devices, block_values, pattern):
    rb, _, bs, _ = block_values.shape
    pattern = pattern.T
    over = [(i, (i + 1 if i % 2 else i - 1) % devices) for i in range(devices)]
    across = [(i, i ^ 1) for i in range(devices)]
    to_outer = lambda x: lax.ppermute(x, "grid", over)
    to_inner = lambda x: lax.ppermute(x, "grid", across)
    low_of = lambda panels: jax.ShapeDtypeStruct((panels, rb * bs, bs), BF16)
    low = low_of(rb)
    high = jax.ShapeDtypeStruct(low.shape, F32)
    full = jax.ShapeDtypeStruct(block_values.shape, BF16)

    def call(kernel, operands, outs, scratch=(), into=None, patterned=True, cost=BRIEF):
        in_specs = [VMEM] * len(operands)
        if patterned:
            operands = (pltpu.with_memory_space_constraint(pattern, pltpu.SMEM), *operands)
            in_specs = [SMEM] + in_specs
        aliases = {}
        if into is not None:
            aliases = {len(operands): 0}
            operands, in_specs = (*operands, into), in_specs + [ANY]
        scratch = [pltpu.VMEM(low.shape, BF16)] * scratch + [pltpu.SemaphoreType.DMA((2 * rb * rb,))] if scratch else []
        return pl.pallas_call(
            functools.partial(kernel, devices, rb, bs),
            out_shape=outs,
            in_specs=in_specs,
            out_specs=[ANY if out is full else VMEM for out in outs],
            scratch_shapes=scratch,
            input_output_aliases=aliases,
            compiler_params=pltpu.CompilerParams(vmem_limit_bytes=VMEM_LIMIT),
            cost_estimate=cost,
            name=kernel.__name__,
        )(*operands)

    first, others, outer, own, inner = pack(devices, pattern, block_values)
    from_first, from_others = to_outer(first), to_outer(others)
    outer_own = to_outer(own)
    from_inner, inner_own = to_inner(inner), to_inner(own)

    (part,) = call(begin_kernel, (outer, from_first), (high,), patterned=False, cost=LONGER)
    from_outer, own_part = call(outer_kernel, (outer, from_first, from_others, part), (low, high), patterned=False, cost=LONGER)
    s_own, s_head = call(square_kernel, (own, inner, from_inner, own_part), (low, low_of(rb - 1)))
    s_outer_head = to_outer(s_head)
    s_inner_own = to_inner(s_own)
    cube_part, inner_part, from_outer_part, outer_part = call(
        early_kernel, (own, inner, outer, from_inner, inner_own, from_outer, s_own), (high,) * 4, 2
    )
    s_from_outer, out_there, slots = call(
        ahead_kernel,
        (outer_own, from_outer, from_outer_part, s_own),
        (low, low_of(1), jax.ShapeDtypeStruct((rb, 8, 128), jnp.int32)),
        cost=BRIEF,
    )
    out_here = to_outer(out_there)
    out, rest = call(
        late_kernel,
        (own, outer, outer_own, s_from_outer, s_own, outer_part, cube_part, inner, s_inner_own, inner_part),
        (full, high),
        3,
        cost=BRIEF,
    )
    (out,) = call(head_kernel, (outer, s_outer_head, rest), (full,), 1, into=out, cost=BRIEF)
    return pl.pallas_call(
        functools.partial(tail_kernel, rb, bs),
        out_shape=full,
        in_specs=[VMEM, VMEM, ANY],
        out_specs=ANY,
        scratch_shapes=[pltpu.SemaphoreType.DMA((rb,))],
        input_output_aliases={2: 0},
        compiler_params=pltpu.CompilerParams(vmem_limit_bytes=VMEM_LIMIT),
        cost_estimate=BRIEF,
        name="tail_kernel",
    )(slots, out_here, out)


def solution(mesh):
    return jax.shard_map(
        functools.partial(local, mesh.shape["grid"]),
        mesh=mesh,
        in_specs=(P(("parts", "grid"), None, None, None), P("parts", None)),
        out_specs=P(("parts", "grid"), None, None, None),
        check_vma=False,
    )
```

```python
import functools

import jax
import jax.numpy as jnp
from jax import lax
from jax.experimental import pallas as pl
from jax.experimental.pallas import tpu as pltpu
from jax.sharding import PartitionSpec as P


F32 = jnp.float32
BF16 = jnp.bfloat16
ANY = pl.BlockSpec(memory_space=pl.ANY)
HBM = pl.BlockSpec(memory_space=pltpu.HBM)
VMEM = pl.BlockSpec(memory_space=pltpu.VMEM)
SMEM = pl.BlockSpec(memory_space=pltpu.SMEM)
BRIEF = pl.CostEstimate(flops=1, bytes_accessed=1, transcendentals=0)
LONGER = pl.CostEstimate(flops=5 * 10**9, bytes_accessed=1, transcendentals=0)
VMEM_LIMIT = 24 * 1024 * 1024


def neighbours(devices):
    me = lax.axis_index("grid")
    odd = lax.rem(me, 2)
    above = lax.rem(me + 1, devices)
    below = lax.rem(me + devices - 1, devices)
    return me, jnp.where(odd == 1, above, below), jnp.where(odd == 1, below, above)


def slot_of(pattern, row, column):
    slot = jnp.int32(-1)
    for s in range(pattern.shape[0]):
        slot = jnp.where(pattern[s, row] == column, s, slot)
    return slot


def panel_product(left, right, c, rb, bs):
    total = jnp.dot(left[0], right[c, pl.ds(0, bs), :], preferred_element_type=F32)
    for k in range(1, rb):
        total += jnp.dot(left[k], right[c, pl.ds(k * bs, bs), :], preferred_element_type=F32)
    return total


def drop_absent(ref, pattern, row_device, column_device, rb, bs, panels=None):
    for r in range(rb):
        for j in range(rb if panels is None else panels):
            slot = slot_of(pattern, row_device * rb + r, column_device * rb + j)

            @pl.when(slot < 0)
            def _():
                ref[j, pl.ds(r * bs, bs), :] = jnp.zeros((bs, bs), ref.dtype)


def place(pattern, held, row, owner, columns, cut, first, rb, bs):
    for j in range(rb):
        slot = slot_of(pattern, owner * rb + row, columns * rb + j)
        block = held[jnp.maximum(slot, 0)]
        cut[j, pl.ds((row - first) * bs, bs), :] = jnp.where(slot >= 0, block, jnp.zeros_like(block))


def first_kernel(devices, rb, bs, pattern_hbm, blocks, cut, pattern, held, pattern_sem, sem):
    fetch = pltpu.make_async_copy(pattern_hbm, pattern, pattern_sem)
    fetch.start()
    load = pltpu.make_async_copy(blocks.at[0], held, sem)
    load.start()
    me, other, _ = neighbours(devices)
    fetch.wait()
    load.wait()
    place(pattern, held, 0, me, other, cut, 0, rb, bs)


def pack_kernel(devices, rb, bs, pattern_hbm, blocks, _, others, *rest):
    cuts, (pattern, held, pattern_sem, sems) = rest[:3], rest[3:]
    fetch = pltpu.make_async_copy(pattern_hbm, pattern, pattern_sem)
    fetch.start()
    loads = [pltpu.make_async_copy(blocks.at[r], held.at[r], sems.at[r]) for r in range(rb)]
    for load in loads:
        load.start()
    people = neighbours(devices)
    me, other, partner = people
    fetch.wait()
    for r in range(rb):
        loads[r].wait()
        for cut, columns in zip(cuts, (other, me, partner)):
            place(pattern, held.at[r], r, me, columns, cut, 0, rb, bs)
    others[...] = cuts[0][:, pl.ds(bs, (rb - 1) * bs), :]


def pack(devices, pattern, blocks):
    rb, slots, bs, _ = blocks.shape
    pattern = pltpu.with_memory_space_constraint(pattern, pltpu.HBM)
    blocks = pltpu.with_memory_space_constraint(blocks, pltpu.HBM)
    cut = lambda rows: jax.ShapeDtypeStruct((rb, rows * bs, bs), blocks.dtype)
    params = pltpu.CompilerParams(vmem_limit_bytes=VMEM_LIMIT)
    first = pl.pallas_call(
        functools.partial(first_kernel, devices, rb, bs),
        out_shape=cut(1),
        in_specs=[ANY, ANY],
        out_specs=VMEM,
        scratch_shapes=[
            pltpu.SMEM(pattern.shape, pattern.dtype),
            pltpu.VMEM(blocks.shape[1:], blocks.dtype),
            pltpu.SemaphoreType.DMA,
            pltpu.SemaphoreType.DMA,
        ],
        compiler_params=params,
        cost_estimate=BRIEF,
        name="first",
    )(pattern, blocks)
    return first, *pl.pallas_call(
        functools.partial(pack_kernel, devices, rb, bs),
        out_shape=[cut(rb - 1), cut(rb), cut(rb), cut(rb)],
        in_specs=[ANY, ANY, ANY],
        out_specs=[VMEM] * 4,
        scratch_shapes=[
            pltpu.SMEM(pattern.shape, pattern.dtype),
            pltpu.VMEM(blocks.shape, blocks.dtype),
            pltpu.SemaphoreType.DMA,
            pltpu.SemaphoreType.DMA((rb,)),
        ],
        compiler_params=params,
        cost_estimate=BRIEF,
        name="pack",
    )(pattern, blocks, first)


def scatter(out, pattern, me, column_device, panels, j, sems, base, rb, bs):
    waits = []
    for r in range(rb):
        slot = slot_of(pattern, me * rb + r, column_device * rb + j)
        copy = pltpu.make_async_copy(
            panels.at[j, pl.ds(r * bs, bs), :], out.at[r, jnp.maximum(slot, 0)], sems.at[base + r * rb + j]
        )
        pl.when(slot >= 0)(copy.start)
        waits.append((slot, copy))
    return waits


def settle(waits):
    for slot, copy in waits:
        pl.when(slot >= 0)(copy.wait)


def begin_kernel(devices, rb, bs, outer, from_first, part):
    @pl.loop(0, rb)
    def _(c):
        part[c] = jnp.dot(outer[0], from_first[c], preferred_element_type=F32)


def outer_kernel(devices, rb, bs, outer, from_first, from_others, part, from_outer, own_part):
    from_outer[:, pl.ds(0, bs), :] = from_first[...]
    from_outer[:, pl.ds(bs, (rb - 1) * bs), :] = from_others[...]

    @pl.loop(0, rb)
    def _(c):
        total = part[c]
        for k in range(1, rb):
            total += jnp.dot(outer[k], from_others[c, pl.ds((k - 1) * bs, bs), :], preferred_element_type=F32)
        own_part[c] = total


def square_kernel(devices, rb, bs, pattern, own, inner, from_inner, own_part, s_own, s_head):
    me, _, _ = neighbours(devices)

    @pl.loop(0, rb)
    def _(c):
        s_own[c] = (
            own_part[c] + panel_product(own, own, c, rb, bs) + panel_product(inner, from_inner, c, rb, bs)
        ).astype(BF16)

    drop_absent(s_own, pattern, me, me, rb, bs)
    s_head[...] = s_own[pl.ds(0, rb - 1)]


def early_kernel(
    devices, rb, bs, pattern, own, inner, outer, from_inner, inner_own, from_outer, s_own,
    cube_part, inner_part, from_outer_part, outer_part, s_inner, s_from_inner, sems,
):
    me, _, partner = neighbours(devices)

    @pl.loop(0, rb)
    def _(c):
        s_inner[c] = (panel_product(own, inner, c, rb, bs) + panel_product(inner, inner_own, c, rb, bs)).astype(BF16)
        s_from_inner[c] = (
            panel_product(from_inner, own, c, rb, bs) + panel_product(inner_own, from_inner, c, rb, bs)
        ).astype(BF16)
        from_outer_part[c] = panel_product(from_outer, own, c, rb, bs)
        outer_part[c] = panel_product(own, outer, c, rb, bs)

    drop_absent(s_inner, pattern, me, partner, rb, bs)
    drop_absent(s_from_inner, pattern, partner, me, rb, bs)

    @pl.loop(0, rb)
    def _(c):
        cube_part[c] = panel_product(own, s_own, c, rb, bs) + panel_product(inner, s_from_inner, c, rb, bs)
        inner_part[c] = 3.0 * s_inner[c].astype(F32) - 2.0 * panel_product(own, s_inner, c, rb, bs)


def ahead_kernel(
    devices, rb, bs, pattern, outer_own, from_outer, from_outer_part, s_own, s_from_outer, out_there, slots
):
    me, other, _ = neighbours(devices)
    last = rb - 1
    for r in range(rb):
        slots[r] = jnp.full(slots.shape[1:], slot_of(pattern, me * rb + r, other * rb + last))

    @pl.loop(0, rb)
    def _(c):
        s_from_outer[c] = (from_outer_part[c] + panel_product(outer_own, from_outer, c, rb, bs)).astype(BF16)

    drop_absent(s_from_outer, pattern, other, me, rb, bs)
    cube = panel_product(outer_own, s_from_outer, last, rb, bs) + panel_product(from_outer, s_own, last, rb, bs)
    out_there[0] = (3.0 * s_from_outer[last].astype(F32) - 2.0 * cube).astype(BF16)


def late_kernel(
    devices, rb, bs, pattern, own, outer, outer_own, s_from_outer, s_own, outer_part, cube_part, inner,
    s_inner_own, inner_part, out, rest, s_outer, out_own, out_inner, sems,
):
    me, other, partner = neighbours(devices)
    waits = []
    for c in range(rb):
        out_inner[c] = (inner_part[c] - 2.0 * panel_product(inner, s_inner_own, c, rb, bs)).astype(BF16)
        waits += scatter(out, pattern, me, partner, out_inner, c, sems, rb * rb, rb, bs)
    for c in range(rb):
        cube = cube_part[c] + panel_product(outer, s_from_outer, c, rb, bs)
        out_own[c] = (3.0 * s_own[c].astype(F32) - 2.0 * cube).astype(BF16)
        waits += scatter(out, pattern, me, me, out_own, c, sems, 0, rb, bs)

    @pl.loop(0, rb - 1)
    def _(c):
        s_outer[c] = (outer_part[c] + panel_product(outer, outer_own, c, rb, bs)).astype(BF16)

    drop_absent(s_outer, pattern, me, other, rb, bs, rb - 1)

    @pl.loop(0, rb - 1)
    def _(c):
        rest[c] = 3.0 * s_outer[c].astype(F32) - 2.0 * panel_product(own, s_outer, c, rb, bs)

    settle(waits)


def head_kernel(devices, rb, bs, pattern, outer, s_outer_head, rest, _, out, out_outer, sems):
    me, other, _ = neighbours(devices)
    waits = []
    for c in range(rb - 1):
        out_outer[c] = (rest[c] - 2.0 * panel_product(outer, s_outer_head, c, rb, bs)).astype(BF16)
        waits += scatter(out, pattern, me, other, out_outer, c, sems, 0, rb, bs)
    settle(waits)


def tail_kernel(rb, bs, slots, panel, _, out, sems):
    waits = []
    for r in range(rb):
        slot = slots[r, 0, 0]
        copy = pltpu.make_async_copy(panel.at[0, pl.ds(r * bs, bs), :], out.at[r, jnp.maximum(slot, 0)], sems.at[r])
        pl.when(slot >= 0)(copy.start)
        waits.append((slot, copy))
    settle(waits)


def local(devices, block_values, pattern):
    rb, _, bs, _ = block_values.shape
    pattern = pattern.T
    over = [(i, (i + 1 if i % 2 else i - 1) % devices) for i in range(devices)]
    across = [(i, i ^ 1) for i in range(devices)]
    to_outer = lambda x: lax.ppermute(x, "grid", over)
    to_inner = lambda x: lax.ppermute(x, "grid", across)
    low_of = lambda panels: jax.ShapeDtypeStruct((panels, rb * bs, bs), BF16)
    low = low_of(rb)
    high = jax.ShapeDtypeStruct(low.shape, F32)
    full = jax.ShapeDtypeStruct(block_values.shape, BF16)

    def call(kernel, operands, outs, scratch=(), into=None, patterned=True, cost=BRIEF):
        in_specs = [VMEM] * len(operands)
        if patterned:
            operands = (pltpu.with_memory_space_constraint(pattern, pltpu.SMEM), *operands)
            in_specs = [SMEM] + in_specs
        aliases = {}
        if into is not None:
            aliases = {len(operands): 0}
            operands, in_specs = (*operands, into), in_specs + [ANY]
        scratch = [pltpu.VMEM(low.shape, BF16)] * scratch + [pltpu.SemaphoreType.DMA((2 * rb * rb,))] if scratch else []
        return pl.pallas_call(
            functools.partial(kernel, devices, rb, bs),
            out_shape=outs,
            in_specs=in_specs,
            out_specs=[ANY if out is full else VMEM for out in outs],
            scratch_shapes=scratch,
            input_output_aliases=aliases,
            compiler_params=pltpu.CompilerParams(vmem_limit_bytes=VMEM_LIMIT),
            cost_estimate=cost,
            name=kernel.__name__,
        )(*operands)

    first, others, outer, own, inner = pack(devices, pattern, block_values)
    from_first, from_others = to_outer(first), to_outer(others)
    outer_own = to_outer(own)
    from_inner, inner_own = to_inner(inner), to_inner(own)

    (part,) = call(begin_kernel, (outer, from_first), (high,), patterned=False, cost=LONGER)
    from_outer, own_part = call(outer_kernel, (outer, from_first, from_others, part), (low, high), patterned=False, cost=LONGER)
    s_own, s_head = call(square_kernel, (own, inner, from_inner, own_part), (low, low_of(rb - 1)))
    s_outer_head = to_outer(s_head)
    s_inner_own = to_inner(s_own)
    cube_part, inner_part, from_outer_part, outer_part = call(
        early_kernel, (own, inner, outer, from_inner, inner_own, from_outer, s_own), (high,) * 4, 2
    )
    s_from_outer, out_there, slots = call(
        ahead_kernel,
        (outer_own, from_outer, from_outer_part, s_own),
        (low, low_of(1), jax.ShapeDtypeStruct((rb, 8, 128), jnp.int32)),
        cost=BRIEF,
    )
    out_here = to_outer(out_there)
    out, rest = call(
        late_kernel,
        (own, outer, outer_own, s_from_outer, s_own, outer_part, cube_part, inner, s_inner_own, inner_part),
        (full, high),
        3,
        cost=BRIEF,
    )
    (out,) = call(head_kernel, (outer, s_outer_head, rest), (full,), 1, into=out, cost=BRIEF)
    return pl.pallas_call(
        functools.partial(tail_kernel, rb, bs),
        out_shape=full,
        in_specs=[VMEM, VMEM, ANY],
        out_specs=ANY,
        scratch_shapes=[pltpu.SemaphoreType.DMA((rb,))],
        input_output_aliases={2: 0},
        compiler_params=pltpu.CompilerParams(vmem_limit_bytes=VMEM_LIMIT),
        cost_estimate=BRIEF,
        name="tail_kernel",
    )(slots, out_here, out)


def solution(mesh):
    return jax.shard_map(
        functools.partial(local, mesh.shape["grid"]),
        mesh=mesh,
        in_specs=(P(("parts", "grid"), None, None, None), P("parts", None)),
        out_specs=P(("parts", "grid"), None, None, None),
        check_vma=False,
    )
```

```python
import functools

import jax
import jax.numpy as jnp
from jax import lax
from jax.experimental import pallas as pl
from jax.experimental.pallas import tpu as pltpu
from jax.sharding import PartitionSpec as P


F32 = jnp.float32
BF16 = jnp.bfloat16
ANY = pl.BlockSpec(memory_space=pl.ANY)
HBM = pl.BlockSpec(memory_space=pltpu.HBM)
VMEM = pl.BlockSpec(memory_space=pltpu.VMEM)
SMEM = pl.BlockSpec(memory_space=pltpu.SMEM)
BRIEF = pl.CostEstimate(flops=1, bytes_accessed=1, transcendentals=0)
LONGER = pl.CostEstimate(flops=5 * 10**9, bytes_accessed=1, transcendentals=0)
LONGEST = pl.CostEstimate(flops=10**10, bytes_accessed=1, transcendentals=0)
VMEM_LIMIT = 24 * 1024 * 1024


def neighbours(devices):
    me = lax.axis_index("grid")
    odd = lax.rem(me, 2)
    above = lax.rem(me + 1, devices)
    below = lax.rem(me + devices - 1, devices)
    return me, jnp.where(odd == 1, above, below), jnp.where(odd == 1, below, above)


def slot_of(pattern, row, column):
    slot = jnp.int32(-1)
    for s in range(pattern.shape[0]):
        slot = jnp.where(pattern[s, row] == column, s, slot)
    return slot


def panel_product(left, right, c, rb, bs):
    total = jnp.dot(left[0], right[c, pl.ds(0, bs), :], preferred_element_type=F32)
    for k in range(1, rb):
        total += jnp.dot(left[k], right[c, pl.ds(k * bs, bs), :], preferred_element_type=F32)
    return total


def drop_absent(ref, pattern, row_device, column_device, rb, bs, panels=None):
    for r in range(rb):
        for j in range(rb if panels is None else panels):
            slot = slot_of(pattern, row_device * rb + r, column_device * rb + j)

            @pl.when(slot < 0)
            def _():
                ref[j, pl.ds(r * bs, bs), :] = jnp.zeros((bs, bs), ref.dtype)


def place(slots, held, cut, start, size):
    for j, slot in enumerate(slots):
        block = held[jnp.maximum(slot, 0)]
        cut[j, pl.ds(start, size), :] = jnp.where(slot >= 0, block, jnp.zeros_like(block))


def first_kernel(devices, rb, bs, pattern_hbm, blocks, cut, pattern, held, pattern_sem, sem):
    fetch = pltpu.make_async_copy(pattern_hbm, pattern, pattern_sem)
    fetch.start()
    load = pltpu.make_async_copy(blocks.at[0, :, pl.ds(0, bs // 2), :], held, sem)
    load.start()
    me, other, _ = neighbours(devices)
    fetch.wait()
    slots = [slot_of(pattern, me * rb, other * rb + j) for j in range(rb)]
    load.wait()
    place(slots, held, cut, 0, bs // 2)


def pack_kernel(devices, rb, bs, pattern_hbm, blocks, _, others, *rest):
    cuts, (pattern, held, pattern_sem, sems) = rest[:3], rest[3:]
    fetch = pltpu.make_async_copy(pattern_hbm, pattern, pattern_sem)
    fetch.start()
    loads = [pltpu.make_async_copy(blocks.at[r], held.at[r], sems.at[r]) for r in range(rb)]
    for load in loads:
        load.start()
    people = neighbours(devices)
    me, other, partner = people
    fetch.wait()
    for r in range(rb):
        loads[r].wait()
        for cut, columns in zip(cuts, (other, me, partner)):
            slots = [slot_of(pattern, me * rb + r, columns * rb + j) for j in range(rb)]
            place(slots, held.at[r], cut, r * bs, bs)
    others[...] = cuts[0][:, pl.ds(bs // 2, rb * bs - bs // 2), :]


def pack(devices, pattern, blocks):
    rb, slots, bs, _ = blocks.shape
    pattern = pltpu.with_memory_space_constraint(pattern, pltpu.HBM)
    blocks = pltpu.with_memory_space_constraint(blocks, pltpu.HBM)
    cut = lambda rows: jax.ShapeDtypeStruct((rb, rows, bs), blocks.dtype)
    params = pltpu.CompilerParams(vmem_limit_bytes=VMEM_LIMIT)
    first = pl.pallas_call(
        functools.partial(first_kernel, devices, rb, bs),
        out_shape=cut(bs // 2),
        in_specs=[ANY, ANY],
        out_specs=VMEM,
        scratch_shapes=[
            pltpu.SMEM(pattern.shape, pattern.dtype),
            pltpu.VMEM((slots, bs // 2, bs), blocks.dtype),
            pltpu.SemaphoreType.DMA,
            pltpu.SemaphoreType.DMA,
        ],
        compiler_params=params,
        cost_estimate=BRIEF,
        name="first",
    )(pattern, blocks)
    return first, *pl.pallas_call(
        functools.partial(pack_kernel, devices, rb, bs),
        out_shape=[cut(rb * bs - bs // 2)] + [cut(rb * bs)] * 3,
        in_specs=[ANY, ANY, ANY],
        out_specs=[VMEM] * 4,
        scratch_shapes=[
            pltpu.SMEM(pattern.shape, pattern.dtype),
            pltpu.VMEM(blocks.shape, blocks.dtype),
            pltpu.SemaphoreType.DMA,
            pltpu.SemaphoreType.DMA((rb,)),
        ],
        compiler_params=params,
        cost_estimate=BRIEF,
        name="pack",
    )(pattern, blocks, first)


def scatter(out, pattern, me, column_device, panels, j, sems, base, rb, bs):
    waits = []
    for r in range(rb):
        slot = slot_of(pattern, me * rb + r, column_device * rb + j)
        copy = pltpu.make_async_copy(
            panels.at[j, pl.ds(r * bs, bs), :], out.at[r, jnp.maximum(slot, 0)], sems.at[base + r * rb + j]
        )
        pl.when(slot >= 0)(copy.start)
        waits.append((slot, copy))
    return waits


def settle(waits):
    for slot, copy in waits:
        pl.when(slot >= 0)(copy.wait)


def begin_kernel(devices, rb, bs, outer, from_first, part):
    @pl.loop(0, rb)
    def _(c):
        part[c] = jnp.dot(outer[0, :, pl.ds(0, bs // 2)], from_first[c], preferred_element_type=F32)


def outer_kernel(devices, rb, bs, outer, from_first, from_others, part, from_outer, own_part):
    half = bs // 2
    from_outer[:, pl.ds(0, half), :] = from_first[...]
    from_outer[:, pl.ds(half, rb * bs - half), :] = from_others[...]

    @pl.loop(0, rb)
    def _(c):
        total = part[c] + jnp.dot(
            outer[0, :, pl.ds(half, half)], from_others[c, pl.ds(0, half), :], preferred_element_type=F32
        )
        for k in range(1, rb):
            rows = pl.ds(k * bs - half, bs)
            total += jnp.dot(outer[k], from_others[c, rows, :], preferred_element_type=F32)
        own_part[c] = total


def square_kernel(devices, rb, bs, pattern, own, inner, from_inner, own_part, s_own, s_head):
    me, _, _ = neighbours(devices)

    @pl.loop(0, rb)
    def _(c):
        s_own[c] = (
            own_part[c] + panel_product(own, own, c, rb, bs) + panel_product(inner, from_inner, c, rb, bs)
        ).astype(BF16)

    drop_absent(s_own, pattern, me, me, rb, bs)
    s_head[...] = s_own[pl.ds(0, rb - 1)]


def early_kernel(
    devices, rb, bs, pattern, own, inner, outer, from_inner, inner_own, from_outer, s_own,
    cube_part, inner_part, from_outer_part, outer_part, s_inner, s_from_inner, sems,
):
    me, _, partner = neighbours(devices)

    @pl.loop(0, rb)
    def _(c):
        s_inner[c] = (panel_product(own, inner, c, rb, bs) + panel_product(inner, inner_own, c, rb, bs)).astype(BF16)
        s_from_inner[c] = (
            panel_product(from_inner, own, c, rb, bs) + panel_product(inner_own, from_inner, c, rb, bs)
        ).astype(BF16)
        from_outer_part[c] = panel_product(from_outer, own, c, rb, bs)
        outer_part[c] = panel_product(own, outer, c, rb, bs)

    drop_absent(s_inner, pattern, me, partner, rb, bs)
    drop_absent(s_from_inner, pattern, partner, me, rb, bs)

    @pl.loop(0, rb)
    def _(c):
        cube_part[c] = panel_product(own, s_own, c, rb, bs) + panel_product(inner, s_from_inner, c, rb, bs)
        inner_part[c] = 3.0 * s_inner[c].astype(F32) - 2.0 * panel_product(own, s_inner, c, rb, bs)


def ahead_kernel(
    devices, rb, bs, pattern, outer_own, from_outer, from_outer_part, s_own, s_from_outer, out_most, out_last, slots
):
    me, other, _ = neighbours(devices)
    last = rb - 1
    for r in range(rb):
        slots[r] = jnp.full(slots.shape[1:], slot_of(pattern, me * rb + r, other * rb + last))

    @pl.loop(0, rb)
    def _(c):
        s_from_outer[c] = (from_outer_part[c] + panel_product(outer_own, from_outer, c, rb, bs)).astype(BF16)

    drop_absent(s_from_outer, pattern, other, me, rb, bs)
    cube = panel_product(outer_own, s_from_outer, last, rb, bs) + panel_product(from_outer, s_own, last, rb, bs)
    out_there = (3.0 * s_from_outer[last].astype(F32) - 2.0 * cube).astype(BF16)
    out_most[...] = out_there[: last * bs]
    out_last[...] = out_there[last * bs :]


def late_kernel(
    devices, rb, bs, pattern, own, outer, outer_own, s_from_outer, s_own, outer_part, cube_part, inner,
    s_inner_own, inner_part, out, rest, s_outer, out_own, out_inner, sems,
):
    me, other, partner = neighbours(devices)
    waits = []
    for c in range(rb):
        out_inner[c] = (inner_part[c] - 2.0 * panel_product(inner, s_inner_own, c, rb, bs)).astype(BF16)
        waits += scatter(out, pattern, me, partner, out_inner, c, sems, rb * rb, rb, bs)
    for c in range(rb):
        cube = cube_part[c] + panel_product(outer, s_from_outer, c, rb, bs)
        out_own[c] = (3.0 * s_own[c].astype(F32) - 2.0 * cube).astype(BF16)
        waits += scatter(out, pattern, me, me, out_own, c, sems, 0, rb, bs)

    @pl.loop(0, rb - 1)
    def _(c):
        s_outer[c] = (outer_part[c] + panel_product(outer, outer_own, c, rb, bs)).astype(BF16)

    drop_absent(s_outer, pattern, me, other, rb, bs, rb - 1)

    @pl.loop(0, rb - 1)
    def _(c):
        rest[c] = 3.0 * s_outer[c].astype(F32) - 2.0 * panel_product(own, s_outer, c, rb, bs)

    settle(waits)


def head_kernel(devices, rb, bs, pattern, outer, s_outer_head, rest, _, out, out_outer, sems):
    me, other, _ = neighbours(devices)
    waits = []
    for c in range(rb - 1):
        out_outer[c] = (rest[c] - 2.0 * panel_product(outer, s_outer_head, c, rb, bs)).astype(BF16)
        waits += scatter(out, pattern, me, other, out_outer, c, sems, 0, rb, bs)
    settle(waits)


def tail_kernel(first, bs, slots, blocks, _, out, sems):
    waits = []
    for r in range(blocks.shape[0] // bs):
        slot = slots[first + r, 0, 0]
        copy = pltpu.make_async_copy(
            blocks.at[pl.ds(r * bs, bs), :], out.at[first + r, jnp.maximum(slot, 0)], sems.at[r]
        )
        pl.when(slot >= 0)(copy.start)
        waits.append((slot, copy))
    settle(waits)


def local(devices, block_values, pattern):
    rb, _, bs, _ = block_values.shape
    pattern = pattern.T
    over = [(i, (i + 1 if i % 2 else i - 1) % devices) for i in range(devices)]
    across = [(i, i ^ 1) for i in range(devices)]
    to_outer = lambda x: lax.ppermute(x, "grid", over)
    to_inner = lambda x: lax.ppermute(x, "grid", across)
    low_of = lambda panels: jax.ShapeDtypeStruct((panels, rb * bs, bs), BF16)
    low = low_of(rb)
    high = jax.ShapeDtypeStruct(low.shape, F32)
    full = jax.ShapeDtypeStruct(block_values.shape, BF16)

    def call(kernel, operands, outs, scratch=(), into=None, patterned=True, cost=BRIEF):
        in_specs = [VMEM] * len(operands)
        if patterned:
            operands = (pltpu.with_memory_space_constraint(pattern, pltpu.SMEM), *operands)
            in_specs = [SMEM] + in_specs
        aliases = {}
        if into is not None:
            aliases = {len(operands): 0}
            operands, in_specs = (*operands, into), in_specs + [ANY]
        scratch = [pltpu.VMEM(low.shape, BF16)] * scratch + [pltpu.SemaphoreType.DMA((2 * rb * rb,))] if scratch else []
        return pl.pallas_call(
            functools.partial(kernel, devices, rb, bs),
            out_shape=outs,
            in_specs=in_specs,
            out_specs=[ANY if out is full else VMEM for out in outs],
            scratch_shapes=scratch,
            input_output_aliases=aliases,
            compiler_params=pltpu.CompilerParams(vmem_limit_bytes=VMEM_LIMIT),
            cost_estimate=cost,
            name=kernel.__name__,
        )(*operands)

    first, others, outer, own, inner = pack(devices, pattern, block_values)
    from_first, from_others = to_outer(first), to_outer(others)
    outer_own = to_outer(own)
    from_inner, inner_own = to_inner(inner), to_inner(own)

    (part,) = call(begin_kernel, (outer, from_first), (high,), patterned=False, cost=LONGEST)
    from_outer, own_part = call(outer_kernel, (outer, from_first, from_others, part), (low, high), patterned=False, cost=LONGER)
    s_own, s_head = call(square_kernel, (own, inner, from_inner, own_part), (low, low_of(rb - 1)))
    s_outer_head = to_outer(s_head)
    s_inner_own = to_inner(s_own)
    cube_part, inner_part, from_outer_part, outer_part = call(
        early_kernel, (own, inner, outer, from_inner, inner_own, from_outer, s_own), (high,) * 4, 2
    )
    s_from_outer, out_most, out_last, slots = call(
        ahead_kernel,
        (outer_own, from_outer, from_outer_part, s_own),
        (
            low,
            jax.ShapeDtypeStruct(((rb - 1) * bs, bs), BF16),
            jax.ShapeDtypeStruct((bs, bs), BF16),
            jax.ShapeDtypeStruct((rb, 8, 128), jnp.int32),
        ),
        cost=BRIEF,
    )
    arrivals = to_outer(out_most), to_outer(out_last)
    out, rest = call(
        late_kernel,
        (own, outer, outer_own, s_from_outer, s_own, outer_part, cube_part, inner, s_inner_own, inner_part),
        (full, high),
        3,
        cost=BRIEF,
    )
    (out,) = call(head_kernel, (outer, s_outer_head, rest), (full,), 1, into=out, cost=BRIEF)
    for first, blocks in zip((0, rb - 1), arrivals):
        out = pl.pallas_call(
            functools.partial(tail_kernel, first, bs),
            out_shape=full,
            in_specs=[VMEM, VMEM, ANY],
            out_specs=ANY,
            scratch_shapes=[pltpu.SemaphoreType.DMA((blocks.shape[0] // bs,))],
            input_output_aliases={2: 0},
            compiler_params=pltpu.CompilerParams(vmem_limit_bytes=VMEM_LIMIT),
            cost_estimate=BRIEF,
            name="tail_kernel",
        )(slots, blocks, out)
    return out


def solution(mesh):
    return jax.shard_map(
        functools.partial(local, mesh.shape["grid"]),
        mesh=mesh,
        in_specs=(P(("parts", "grid"), None, None, None), P("parts", None)),
        out_specs=P(("parts", "grid"), None, None, None),
        check_vma=False,
    )
```

```python
import functools

import jax
import jax.numpy as jnp
from jax import lax
from jax.experimental import pallas as pl
from jax.experimental.pallas import tpu as pltpu
from jax.sharding import PartitionSpec as P


F32 = jnp.float32
BF16 = jnp.bfloat16
ANY = pl.BlockSpec(memory_space=pl.ANY)
HBM = pl.BlockSpec(memory_space=pltpu.HBM)
VMEM = pl.BlockSpec(memory_space=pltpu.VMEM)
SMEM = pl.BlockSpec(memory_space=pltpu.SMEM)
BRIEF = pl.CostEstimate(flops=1, bytes_accessed=1, transcendentals=0)
LONGER = pl.CostEstimate(flops=5 * 10**9, bytes_accessed=1, transcendentals=0)
LONGEST = pl.CostEstimate(flops=8 * 10**9, bytes_accessed=1, transcendentals=0)
VMEM_LIMIT = 24 * 1024 * 1024


def neighbours(devices):
    me = lax.axis_index("grid")
    odd = lax.rem(me, 2)
    above = lax.rem(me + 1, devices)
    below = lax.rem(me + devices - 1, devices)
    return me, jnp.where(odd == 1, above, below), jnp.where(odd == 1, below, above)


def slot_of(pattern, row, column):
    slot = jnp.int32(-1)
    for s in range(pattern.shape[0]):
        slot = jnp.where(pattern[s, row] == column, s, slot)
    return slot


def panel_product(left, right, c, rb, bs):
    total = jnp.dot(left[0], right[c, pl.ds(0, bs), :], preferred_element_type=F32)
    for k in range(1, rb):
        total += jnp.dot(left[k], right[c, pl.ds(k * bs, bs), :], preferred_element_type=F32)
    return total


def drop_absent(ref, pattern, row_device, column_device, rb, bs, panels=None):
    for r in range(rb):
        for j in range(rb if panels is None else panels):
            slot = slot_of(pattern, row_device * rb + r, column_device * rb + j)

            @pl.when(slot < 0)
            def _():
                ref[j, pl.ds(r * bs, bs), :] = jnp.zeros((bs, bs), ref.dtype)


def place(slots, held, cut, start, size):
    for j, slot in enumerate(slots):
        block = held[jnp.maximum(slot, 0)]
        cut[j, pl.ds(start, size), :] = jnp.where(slot >= 0, block, jnp.zeros_like(block))


def first_kernel(devices, rb, bs, pattern_hbm, blocks, cut, pattern, held, pattern_sem, sem):
    fetch = pltpu.make_async_copy(pattern_hbm, pattern, pattern_sem)
    fetch.start()
    load = pltpu.make_async_copy(blocks.at[0, :, pl.ds(0, bs * 5 // 8), :], held, sem)
    load.start()
    me, other, _ = neighbours(devices)
    fetch.wait()
    slots = [slot_of(pattern, me * rb, other * rb + j) for j in range(rb)]
    load.wait()
    place(slots, held, cut, 0, bs * 5 // 8)


def pack_kernel(devices, rb, bs, pattern_hbm, blocks, _, others, *rest):
    cuts, (pattern, held, pattern_sem, sems) = rest[:3], rest[3:]
    fetch = pltpu.make_async_copy(pattern_hbm, pattern, pattern_sem)
    fetch.start()
    loads = [pltpu.make_async_copy(blocks.at[r], held.at[r], sems.at[r]) for r in range(rb)]
    for load in loads:
        load.start()
    people = neighbours(devices)
    me, other, partner = people
    fetch.wait()
    for r in range(rb):
        loads[r].wait()
        for cut, columns in zip(cuts, (other, me, partner)):
            slots = [slot_of(pattern, me * rb + r, columns * rb + j) for j in range(rb)]
            place(slots, held.at[r], cut, r * bs, bs)
    others[...] = cuts[0][:, pl.ds(bs * 5 // 8, rb * bs - bs * 5 // 8), :]


def pack(devices, pattern, blocks):
    rb, slots, bs, _ = blocks.shape
    pattern = pltpu.with_memory_space_constraint(pattern, pltpu.HBM)
    blocks = pltpu.with_memory_space_constraint(blocks, pltpu.HBM)
    cut = lambda rows: jax.ShapeDtypeStruct((rb, rows, bs), blocks.dtype)
    params = pltpu.CompilerParams(vmem_limit_bytes=VMEM_LIMIT)
    first = pl.pallas_call(
        functools.partial(first_kernel, devices, rb, bs),
        out_shape=cut(bs * 5 // 8),
        in_specs=[ANY, ANY],
        out_specs=VMEM,
        scratch_shapes=[
            pltpu.SMEM(pattern.shape, pattern.dtype),
            pltpu.VMEM((slots, bs * 5 // 8, bs), blocks.dtype),
            pltpu.SemaphoreType.DMA,
            pltpu.SemaphoreType.DMA,
        ],
        compiler_params=params,
        cost_estimate=BRIEF,
        name="first",
    )(pattern, blocks)
    return first, *pl.pallas_call(
        functools.partial(pack_kernel, devices, rb, bs),
        out_shape=[cut(rb * bs - bs * 5 // 8)] + [cut(rb * bs)] * 3,
        in_specs=[ANY, ANY, ANY],
        out_specs=[VMEM] * 4,
        scratch_shapes=[
            pltpu.SMEM(pattern.shape, pattern.dtype),
            pltpu.VMEM(blocks.shape, blocks.dtype),
            pltpu.SemaphoreType.DMA,
            pltpu.SemaphoreType.DMA((rb,)),
        ],
        compiler_params=params,
        cost_estimate=BRIEF,
        name="pack",
    )(pattern, blocks, first)


def scatter(out, pattern, me, column_device, panels, j, sems, base, rb, bs):
    waits = []
    for r in range(rb):
        slot = slot_of(pattern, me * rb + r, column_device * rb + j)
        copy = pltpu.make_async_copy(
            panels.at[j, pl.ds(r * bs, bs), :], out.at[r, jnp.maximum(slot, 0)], sems.at[base + r * rb + j]
        )
        pl.when(slot >= 0)(copy.start)
        waits.append((slot, copy))
    return waits


def settle(waits):
    for slot, copy in waits:
        pl.when(slot >= 0)(copy.wait)


def begin_kernel(devices, rb, bs, from_first, held):
    held[...] = from_first[...]


def outer_kernel(devices, rb, bs, outer, held, from_others, from_outer, own_part):
    size = held.shape[1]
    from_outer[:, pl.ds(0, size), :] = held[...]
    from_outer[:, pl.ds(size, rb * bs - size), :] = from_others[...]

    @pl.loop(0, rb)
    def _(c):
        own_part[c] = panel_product(outer, from_outer, c, rb, bs)


def square_kernel(devices, rb, bs, pattern, own, inner, from_inner, own_part, s_own, s_head):
    me, _, _ = neighbours(devices)

    @pl.loop(0, rb)
    def _(c):
        s_own[c] = (
            own_part[c] + panel_product(own, own, c, rb, bs) + panel_product(inner, from_inner, c, rb, bs)
        ).astype(BF16)

    drop_absent(s_own, pattern, me, me, rb, bs)
    s_head[...] = s_own[pl.ds(0, rb - 1)]


def early_kernel(
    devices, rb, bs, pattern, own, inner, outer, from_inner, inner_own, from_outer, s_own,
    cube_part, inner_part, from_outer_part, outer_part, s_inner, s_from_inner, sems,
):
    me, _, partner = neighbours(devices)

    @pl.loop(0, rb)
    def _(c):
        s_inner[c] = (panel_product(own, inner, c, rb, bs) + panel_product(inner, inner_own, c, rb, bs)).astype(BF16)
        s_from_inner[c] = (
            panel_product(from_inner, own, c, rb, bs) + panel_product(inner_own, from_inner, c, rb, bs)
        ).astype(BF16)
        from_outer_part[c] = panel_product(from_outer, own, c, rb, bs)
        outer_part[c] = panel_product(own, outer, c, rb, bs)

    drop_absent(s_inner, pattern, me, partner, rb, bs)
    drop_absent(s_from_inner, pattern, partner, me, rb, bs)

    @pl.loop(0, rb)
    def _(c):
        cube_part[c] = panel_product(own, s_own, c, rb, bs) + panel_product(inner, s_from_inner, c, rb, bs)
        inner_part[c] = 3.0 * s_inner[c].astype(F32) - 2.0 * panel_product(own, s_inner, c, rb, bs)


def ahead_kernel(
    devices, rb, bs, pattern, outer_own, from_outer, from_outer_part, s_own, s_from_outer, out_most, out_last, slots
):
    me, other, _ = neighbours(devices)
    last = rb - 1
    for r in range(rb):
        slots[r] = jnp.full(slots.shape[1:], slot_of(pattern, me * rb + r, other * rb + last))

    @pl.loop(0, rb)
    def _(c):
        s_from_outer[c] = (from_outer_part[c] + panel_product(outer_own, from_outer, c, rb, bs)).astype(BF16)

    drop_absent(s_from_outer, pattern, other, me, rb, bs)
    cube = panel_product(outer_own, s_from_outer, last, rb, bs) + panel_product(from_outer, s_own, last, rb, bs)
    out_there = (3.0 * s_from_outer[last].astype(F32) - 2.0 * cube).astype(BF16)
    out_most[...] = out_there[: last * bs]
    out_last[...] = out_there[last * bs :]


def late_kernel(
    devices, rb, bs, pattern, own, outer, outer_own, s_from_outer, s_own, outer_part, cube_part, inner,
    s_inner_own, inner_part, out, rest, s_outer, out_own, out_inner, sems,
):
    me, other, partner = neighbours(devices)
    waits = []
    for c in range(rb):
        out_inner[c] = (inner_part[c] - 2.0 * panel_product(inner, s_inner_own, c, rb, bs)).astype(BF16)
        waits += scatter(out, pattern, me, partner, out_inner, c, sems, rb * rb, rb, bs)
    for c in range(rb):
        cube = cube_part[c] + panel_product(outer, s_from_outer, c, rb, bs)
        out_own[c] = (3.0 * s_own[c].astype(F32) - 2.0 * cube).astype(BF16)
        waits += scatter(out, pattern, me, me, out_own, c, sems, 0, rb, bs)

    @pl.loop(0, rb - 1)
    def _(c):
        s_outer[c] = (outer_part[c] + panel_product(outer, outer_own, c, rb, bs)).astype(BF16)

    drop_absent(s_outer, pattern, me, other, rb, bs, rb - 1)

    @pl.loop(0, rb - 1)
    def _(c):
        rest[c] = 3.0 * s_outer[c].astype(F32) - 2.0 * panel_product(own, s_outer, c, rb, bs)

    settle(waits)


def head_kernel(devices, rb, bs, pattern, outer, s_outer_head, rest, _, out, out_outer, sems):
    me, other, _ = neighbours(devices)
    waits = []
    for c in range(rb - 1):
        out_outer[c] = (rest[c] - 2.0 * panel_product(outer, s_outer_head, c, rb, bs)).astype(BF16)
        waits += scatter(out, pattern, me, other, out_outer, c, sems, 0, rb, bs)
    settle(waits)


def tail_kernel(first, bs, slots, blocks, _, out, sems):
    waits = []
    for r in range(blocks.shape[0] // bs):
        slot = slots[first + r, 0, 0]
        copy = pltpu.make_async_copy(
            blocks.at[pl.ds(r * bs, bs), :], out.at[first + r, jnp.maximum(slot, 0)], sems.at[r]
        )
        pl.when(slot >= 0)(copy.start)
        waits.append((slot, copy))
    settle(waits)


def local(devices, block_values, pattern):
    rb, _, bs, _ = block_values.shape
    pattern = pattern.T
    over = [(i, (i + 1 if i % 2 else i - 1) % devices) for i in range(devices)]
    across = [(i, i ^ 1) for i in range(devices)]
    to_outer = lambda x: lax.ppermute(x, "grid", over)
    to_inner = lambda x: lax.ppermute(x, "grid", across)
    low_of = lambda panels: jax.ShapeDtypeStruct((panels, rb * bs, bs), BF16)
    low = low_of(rb)
    high = jax.ShapeDtypeStruct(low.shape, F32)
    full = jax.ShapeDtypeStruct(block_values.shape, BF16)

    def call(kernel, operands, outs, scratch=(), into=None, patterned=True, cost=BRIEF):
        in_specs = [VMEM] * len(operands)
        if patterned:
            operands = (pltpu.with_memory_space_constraint(pattern, pltpu.SMEM), *operands)
            in_specs = [SMEM] + in_specs
        aliases = {}
        if into is not None:
            aliases = {len(operands): 0}
            operands, in_specs = (*operands, into), in_specs + [ANY]
        scratch = [pltpu.VMEM(low.shape, BF16)] * scratch + [pltpu.SemaphoreType.DMA((2 * rb * rb,))] if scratch else []
        return pl.pallas_call(
            functools.partial(kernel, devices, rb, bs),
            out_shape=outs,
            in_specs=in_specs,
            out_specs=[ANY if out is full else VMEM for out in outs],
            scratch_shapes=scratch,
            input_output_aliases=aliases,
            compiler_params=pltpu.CompilerParams(vmem_limit_bytes=VMEM_LIMIT),
            cost_estimate=cost,
            name=kernel.__name__,
        )(*operands)

    first, others, outer, own, inner = pack(devices, pattern, block_values)
    from_first, from_others = to_outer(first), to_outer(others)
    outer_own = to_outer(own)
    from_inner, inner_own = to_inner(inner), to_inner(own)

    (held,) = call(
        begin_kernel, (from_first,), (jax.ShapeDtypeStruct(first.shape, BF16),), patterned=False, cost=LONGEST
    )
    from_outer, own_part = call(outer_kernel, (outer, held, from_others), (low, high), patterned=False, cost=LONGER)
    s_own, s_head = call(square_kernel, (own, inner, from_inner, own_part), (low, low_of(rb - 1)))
    s_outer_head = to_outer(s_head)
    s_inner_own = to_inner(s_own)
    cube_part, inner_part, from_outer_part, outer_part = call(
        early_kernel, (own, inner, outer, from_inner, inner_own, from_outer, s_own), (high,) * 4, 2
    )
    s_from_outer, out_most, out_last, slots = call(
        ahead_kernel,
        (outer_own, from_outer, from_outer_part, s_own),
        (
            low,
            jax.ShapeDtypeStruct(((rb - 1) * bs, bs), BF16),
            jax.ShapeDtypeStruct((bs, bs), BF16),
            jax.ShapeDtypeStruct((rb, 8, 128), jnp.int32),
        ),
        cost=BRIEF,
    )
    arrivals = to_outer(out_most), to_outer(out_last)
    out, rest = call(
        late_kernel,
        (own, outer, outer_own, s_from_outer, s_own, outer_part, cube_part, inner, s_inner_own, inner_part),
        (full, high),
        3,
        cost=BRIEF,
    )
    (out,) = call(head_kernel, (outer, s_outer_head, rest), (full,), 1, into=out, cost=BRIEF)
    for first, blocks in zip((0, rb - 1), arrivals):
        out = pl.pallas_call(
            functools.partial(tail_kernel, first, bs),
            out_shape=full,
            in_specs=[VMEM, VMEM, ANY],
            out_specs=ANY,
            scratch_shapes=[pltpu.SemaphoreType.DMA((blocks.shape[0] // bs,))],
            input_output_aliases={2: 0},
            compiler_params=pltpu.CompilerParams(vmem_limit_bytes=VMEM_LIMIT),
            cost_estimate=BRIEF,
            name="tail_kernel",
        )(slots, blocks, out)
    return out


def solution(mesh):
    return jax.shard_map(
        functools.partial(local, mesh.shape["grid"]),
        mesh=mesh,
        in_specs=(P(("parts", "grid"), None, None, None), P("parts", None)),
        out_specs=P(("parts", "grid"), None, None, None),
        check_vma=False,
    )
```

```python
import functools

import jax
import jax.numpy as jnp
from jax import lax
from jax.experimental import pallas as pl
from jax.experimental.pallas import tpu as pltpu
from jax.sharding import PartitionSpec as P


F32 = jnp.float32
BF16 = jnp.bfloat16
ANY = pl.BlockSpec(memory_space=pl.ANY)
HBM = pl.BlockSpec(memory_space=pltpu.HBM)
VMEM = pl.BlockSpec(memory_space=pltpu.VMEM)
SMEM = pl.BlockSpec(memory_space=pltpu.SMEM)
BRIEF = pl.CostEstimate(flops=1, bytes_accessed=1, transcendentals=0)
LONGER = pl.CostEstimate(flops=5 * 10**9, bytes_accessed=1, transcendentals=0)
LONGEST = pl.CostEstimate(flops=10**10, bytes_accessed=1, transcendentals=0)
VMEM_LIMIT = 24 * 1024 * 1024


def neighbours(devices):
    me = lax.axis_index("grid")
    odd = lax.rem(me, 2)
    above = lax.rem(me + 1, devices)
    below = lax.rem(me + devices - 1, devices)
    return me, jnp.where(odd == 1, above, below), jnp.where(odd == 1, below, above)


def slot_of(pattern, row, column):
    slot = jnp.int32(-1)
    for s in range(pattern.shape[0]):
        slot = jnp.where(pattern[s, row] == column, s, slot)
    return slot


def panel_product(left, right, c, rb, bs):
    total = jnp.dot(left[0], right[c, pl.ds(0, bs), :], preferred_element_type=F32)
    for k in range(1, rb):
        total += jnp.dot(left[k], right[c, pl.ds(k * bs, bs), :], preferred_element_type=F32)
    return total


def drop_absent(ref, pattern, row_device, column_device, rb, bs, panels=None):
    for r in range(rb):
        for j in range(rb if panels is None else panels):
            slot = slot_of(pattern, row_device * rb + r, column_device * rb + j)

            @pl.when(slot < 0)
            def _():
                ref[j, pl.ds(r * bs, bs), :] = jnp.zeros((bs, bs), ref.dtype)


def place(slots, held, cut, start, size):
    for j, slot in enumerate(slots):
        block = held[jnp.maximum(slot, 0)]
        cut[j, pl.ds(start, size), :] = jnp.where(slot >= 0, block, jnp.zeros_like(block))


def first_kernel(devices, rb, bs, pattern_hbm, blocks, cut, pattern, held, pattern_sem, sem):
    fetch = pltpu.make_async_copy(pattern_hbm, pattern, pattern_sem)
    fetch.start()
    load = pltpu.make_async_copy(blocks.at[0, :, pl.ds(0, bs // 2), :], held, sem)
    load.start()
    me, other, _ = neighbours(devices)
    fetch.wait()
    table = pattern[...]
    slot_ids = lax.broadcasted_iota(jnp.int32, table.shape, 0)
    at_row = lax.broadcasted_iota(jnp.int32, table.shape, 1) == me * rb
    slots = [jnp.max(jnp.where(at_row & (table == other * rb + j), slot_ids, -1)) for j in range(rb)]
    load.wait()
    place(slots, held, cut, 0, bs // 2)


def pack_kernel(devices, rb, bs, pattern_hbm, blocks, _, others, *rest):
    cuts, (pattern, held, pattern_sem, sems) = rest[:3], rest[3:]
    fetch = pltpu.make_async_copy(pattern_hbm, pattern, pattern_sem)
    fetch.start()
    loads = [pltpu.make_async_copy(blocks.at[r], held.at[r], sems.at[r]) for r in range(rb)]
    for load in loads:
        load.start()
    people = neighbours(devices)
    me, other, partner = people
    fetch.wait()
    for r in range(rb):
        loads[r].wait()
        for cut, columns in zip(cuts, (other, me, partner)):
            slots = [slot_of(pattern, me * rb + r, columns * rb + j) for j in range(rb)]
            place(slots, held.at[r], cut, r * bs, bs)
    others[...] = cuts[0][:, pl.ds(bs // 2, rb * bs - bs // 2), :]


def pack(devices, pattern, blocks):
    rb, slots, bs, _ = blocks.shape
    pattern = pltpu.with_memory_space_constraint(pattern, pltpu.HBM)
    blocks = pltpu.with_memory_space_constraint(blocks, pltpu.HBM)
    cut = lambda rows: jax.ShapeDtypeStruct((rb, rows, bs), blocks.dtype)
    params = pltpu.CompilerParams(vmem_limit_bytes=VMEM_LIMIT)
    first = pl.pallas_call(
        functools.partial(first_kernel, devices, rb, bs),
        out_shape=cut(bs // 2),
        in_specs=[ANY, ANY],
        out_specs=VMEM,
        scratch_shapes=[
            pltpu.VMEM(pattern.shape, pattern.dtype),
            pltpu.VMEM((slots, bs // 2, bs), blocks.dtype),
            pltpu.SemaphoreType.DMA,
            pltpu.SemaphoreType.DMA,
        ],
        compiler_params=params,
        cost_estimate=BRIEF,
        name="first",
    )(pattern, blocks)
    return first, *pl.pallas_call(
        functools.partial(pack_kernel, devices, rb, bs),
        out_shape=[cut(rb * bs - bs // 2)] + [cut(rb * bs)] * 3,
        in_specs=[ANY, ANY, ANY],
        out_specs=[VMEM] * 4,
        scratch_shapes=[
            pltpu.SMEM(pattern.shape, pattern.dtype),
            pltpu.VMEM(blocks.shape, blocks.dtype),
            pltpu.SemaphoreType.DMA,
            pltpu.SemaphoreType.DMA((rb,)),
        ],
        compiler_params=params,
        cost_estimate=BRIEF,
        name="pack",
    )(pattern, blocks, first)


def scatter(out, pattern, me, column_device, panels, j, sems, base, rb, bs):
    waits = []
    for r in range(rb):
        slot = slot_of(pattern, me * rb + r, column_device * rb + j)
        copy = pltpu.make_async_copy(
            panels.at[j, pl.ds(r * bs, bs), :], out.at[r, jnp.maximum(slot, 0)], sems.at[base + r * rb + j]
        )
        pl.when(slot >= 0)(copy.start)
        waits.append((slot, copy))
    return waits


def settle(waits):
    for slot, copy in waits:
        pl.when(slot >= 0)(copy.wait)


def begin_kernel(devices, rb, bs, outer, from_first, part):
    @pl.loop(0, rb)
    def _(c):
        part[c] = jnp.dot(outer[0, :, pl.ds(0, bs // 2)], from_first[c], preferred_element_type=F32)


def outer_kernel(devices, rb, bs, outer, from_first, from_others, part, from_outer, own_part):
    half = bs // 2
    from_outer[:, pl.ds(0, half), :] = from_first[...]
    from_outer[:, pl.ds(half, rb * bs - half), :] = from_others[...]

    @pl.loop(0, rb)
    def _(c):
        total = part[c] + jnp.dot(
            outer[0, :, pl.ds(half, half)], from_others[c, pl.ds(0, half), :], preferred_element_type=F32
        )
        for k in range(1, rb):
            rows = pl.ds(k * bs - half, bs)
            total += jnp.dot(outer[k], from_others[c, rows, :], preferred_element_type=F32)
        own_part[c] = total


def square_kernel(devices, rb, bs, pattern, own, inner, from_inner, own_part, s_own, s_head):
    me, _, _ = neighbours(devices)

    @pl.loop(0, rb)
    def _(c):
        s_own[c] = (
            own_part[c] + panel_product(own, own, c, rb, bs) + panel_product(inner, from_inner, c, rb, bs)
        ).astype(BF16)

    drop_absent(s_own, pattern, me, me, rb, bs)
    s_head[...] = s_own[pl.ds(0, rb - 1)]


def early_kernel(
    devices, rb, bs, pattern, own, inner, outer, from_inner, inner_own, from_outer, s_own,
    cube_part, inner_part, from_outer_part, outer_part, s_inner, s_from_inner, sems,
):
    me, _, partner = neighbours(devices)

    @pl.loop(0, rb)
    def _(c):
        s_inner[c] = (panel_product(own, inner, c, rb, bs) + panel_product(inner, inner_own, c, rb, bs)).astype(BF16)
        s_from_inner[c] = (
            panel_product(from_inner, own, c, rb, bs) + panel_product(inner_own, from_inner, c, rb, bs)
        ).astype(BF16)
        from_outer_part[c] = panel_product(from_outer, own, c, rb, bs)
        outer_part[c] = panel_product(own, outer, c, rb, bs)

    drop_absent(s_inner, pattern, me, partner, rb, bs)
    drop_absent(s_from_inner, pattern, partner, me, rb, bs)

    @pl.loop(0, rb)
    def _(c):
        cube_part[c] = panel_product(own, s_own, c, rb, bs) + panel_product(inner, s_from_inner, c, rb, bs)
        inner_part[c] = 3.0 * s_inner[c].astype(F32) - 2.0 * panel_product(own, s_inner, c, rb, bs)


def ahead_kernel(
    devices, rb, bs, pattern, outer_own, from_outer, from_outer_part, s_own, s_from_outer, out_most, out_last, slots
):
    me, other, _ = neighbours(devices)
    last = rb - 1
    for r in range(rb):
        slots[r] = jnp.full(slots.shape[1:], slot_of(pattern, me * rb + r, other * rb + last))

    @pl.loop(0, rb)
    def _(c):
        s_from_outer[c] = (from_outer_part[c] + panel_product(outer_own, from_outer, c, rb, bs)).astype(BF16)

    drop_absent(s_from_outer, pattern, other, me, rb, bs)
    cube = panel_product(outer_own, s_from_outer, last, rb, bs) + panel_product(from_outer, s_own, last, rb, bs)
    out_there = (3.0 * s_from_outer[last].astype(F32) - 2.0 * cube).astype(BF16)
    out_most[...] = out_there[: last * bs]
    out_last[...] = out_there[last * bs :]


def late_kernel(
    devices, rb, bs, pattern, own, outer, outer_own, s_from_outer, s_own, outer_part, cube_part, inner,
    s_inner_own, inner_part, out, rest, s_outer, out_own, out_inner, sems,
):
    me, other, partner = neighbours(devices)
    waits = []
    for c in range(rb):
        out_inner[c] = (inner_part[c] - 2.0 * panel_product(inner, s_inner_own, c, rb, bs)).astype(BF16)
        waits += scatter(out, pattern, me, partner, out_inner, c, sems, rb * rb, rb, bs)
    for c in range(rb):
        cube = cube_part[c] + panel_product(outer, s_from_outer, c, rb, bs)
        out_own[c] = (3.0 * s_own[c].astype(F32) - 2.0 * cube).astype(BF16)
        waits += scatter(out, pattern, me, me, out_own, c, sems, 0, rb, bs)

    @pl.loop(0, rb - 1)
    def _(c):
        s_outer[c] = (outer_part[c] + panel_product(outer, outer_own, c, rb, bs)).astype(BF16)

    drop_absent(s_outer, pattern, me, other, rb, bs, rb - 1)

    @pl.loop(0, rb - 1)
    def _(c):
        rest[c] = 3.0 * s_outer[c].astype(F32) - 2.0 * panel_product(own, s_outer, c, rb, bs)

    settle(waits)


def head_kernel(devices, rb, bs, pattern, outer, s_outer_head, rest, _, out, out_outer, sems):
    me, other, _ = neighbours(devices)
    waits = []
    for c in range(rb - 1):
        out_outer[c] = (rest[c] - 2.0 * panel_product(outer, s_outer_head, c, rb, bs)).astype(BF16)
        waits += scatter(out, pattern, me, other, out_outer, c, sems, 0, rb, bs)
    settle(waits)


def tail_kernel(first, bs, slots, blocks, _, out, sems):
    waits = []
    for r in range(blocks.shape[0] // bs):
        slot = slots[first + r, 0, 0]
        copy = pltpu.make_async_copy(
            blocks.at[pl.ds(r * bs, bs), :], out.at[first + r, jnp.maximum(slot, 0)], sems.at[r]
        )
        pl.when(slot >= 0)(copy.start)
        waits.append((slot, copy))
    settle(waits)


def local(devices, block_values, pattern):
    rb, _, bs, _ = block_values.shape
    pattern = pattern.T
    over = [(i, (i + 1 if i % 2 else i - 1) % devices) for i in range(devices)]
    across = [(i, i ^ 1) for i in range(devices)]
    to_outer = lambda x: lax.ppermute(x, "grid", over)
    to_inner = lambda x: lax.ppermute(x, "grid", across)
    low_of = lambda panels: jax.ShapeDtypeStruct((panels, rb * bs, bs), BF16)
    low = low_of(rb)
    high = jax.ShapeDtypeStruct(low.shape, F32)
    full = jax.ShapeDtypeStruct(block_values.shape, BF16)

    def call(kernel, operands, outs, scratch=(), into=None, patterned=True, cost=BRIEF):
        in_specs = [VMEM] * len(operands)
        if patterned:
            operands = (pltpu.with_memory_space_constraint(pattern, pltpu.SMEM), *operands)
            in_specs = [SMEM] + in_specs
        aliases = {}
        if into is not None:
            aliases = {len(operands): 0}
            operands, in_specs = (*operands, into), in_specs + [ANY]
        scratch = [pltpu.VMEM(low.shape, BF16)] * scratch + [pltpu.SemaphoreType.DMA((2 * rb * rb,))] if scratch else []
        return pl.pallas_call(
            functools.partial(kernel, devices, rb, bs),
            out_shape=outs,
            in_specs=in_specs,
            out_specs=[ANY if out is full else VMEM for out in outs],
            scratch_shapes=scratch,
            input_output_aliases=aliases,
            compiler_params=pltpu.CompilerParams(vmem_limit_bytes=VMEM_LIMIT),
            cost_estimate=cost,
            name=kernel.__name__,
        )(*operands)

    first, others, outer, own, inner = pack(devices, pattern, block_values)
    from_first, from_others = to_outer(first), to_outer(others)
    outer_own = to_outer(own)
    from_inner, inner_own = to_inner(inner), to_inner(own)

    (part,) = call(begin_kernel, (outer, from_first), (high,), patterned=False, cost=LONGEST)
    from_outer, own_part = call(outer_kernel, (outer, from_first, from_others, part), (low, high), patterned=False, cost=LONGER)
    s_own, s_head = call(square_kernel, (own, inner, from_inner, own_part), (low, low_of(rb - 1)))
    s_outer_head = to_outer(s_head)
    s_inner_own = to_inner(s_own)
    cube_part, inner_part, from_outer_part, outer_part = call(
        early_kernel, (own, inner, outer, from_inner, inner_own, from_outer, s_own), (high,) * 4, 2
    )
    s_from_outer, out_most, out_last, slots = call(
        ahead_kernel,
        (outer_own, from_outer, from_outer_part, s_own),
        (
            low,
            jax.ShapeDtypeStruct(((rb - 1) * bs, bs), BF16),
            jax.ShapeDtypeStruct((bs, bs), BF16),
            jax.ShapeDtypeStruct((rb, 8, 128), jnp.int32),
        ),
        cost=BRIEF,
    )
    arrivals = to_outer(out_most), to_outer(out_last)
    out, rest = call(
        late_kernel,
        (own, outer, outer_own, s_from_outer, s_own, outer_part, cube_part, inner, s_inner_own, inner_part),
        (full, high),
        3,
        cost=BRIEF,
    )
    (out,) = call(head_kernel, (outer, s_outer_head, rest), (full,), 1, into=out, cost=BRIEF)
    for first, blocks in zip((0, rb - 1), arrivals):
        out = pl.pallas_call(
            functools.partial(tail_kernel, first, bs),
            out_shape=full,
            in_specs=[VMEM, VMEM, ANY],
            out_specs=ANY,
            scratch_shapes=[pltpu.SemaphoreType.DMA((blocks.shape[0] // bs,))],
            input_output_aliases={2: 0},
            compiler_params=pltpu.CompilerParams(vmem_limit_bytes=VMEM_LIMIT),
            cost_estimate=BRIEF,
            name="tail_kernel",
        )(slots, blocks, out)
    return out


def solution(mesh):
    return jax.shard_map(
        functools.partial(local, mesh.shape["grid"]),
        mesh=mesh,
        in_specs=(P(("parts", "grid"), None, None, None), P("parts", None)),
        out_specs=P(("parts", "grid"), None, None, None),
        check_vma=False,
    )
```

```python
import functools

import jax
import jax.numpy as jnp
from jax import lax
from jax.experimental import pallas as pl
from jax.experimental.pallas import tpu as pltpu
from jax.sharding import PartitionSpec as P


F32 = jnp.float32
BF16 = jnp.bfloat16
ANY = pl.BlockSpec(memory_space=pl.ANY)
HBM = pl.BlockSpec(memory_space=pltpu.HBM)
VMEM = pl.BlockSpec(memory_space=pltpu.VMEM)
SMEM = pl.BlockSpec(memory_space=pltpu.SMEM)
BRIEF = pl.CostEstimate(flops=1, bytes_accessed=1, transcendentals=0)
LONGER = pl.CostEstimate(flops=5 * 10**9, bytes_accessed=1, transcendentals=0)
LONGEST = pl.CostEstimate(flops=10**10, bytes_accessed=1, transcendentals=0)
VMEM_LIMIT = 24 * 1024 * 1024


def neighbours(devices):
    me = lax.axis_index("grid")
    odd = lax.rem(me, 2)
    above = lax.rem(me + 1, devices)
    below = lax.rem(me + devices - 1, devices)
    return me, jnp.where(odd == 1, above, below), jnp.where(odd == 1, below, above)


def slot_of(pattern, row, column):
    slot = jnp.int32(-1)
    for s in range(pattern.shape[0]):
        slot = jnp.where(pattern[s, row] == column, s, slot)
    return slot


def panel_product(left, right, c, rb, bs):
    total = jnp.dot(left[0], right[c, pl.ds(0, bs), :], preferred_element_type=F32)
    for k in range(1, rb):
        total += jnp.dot(left[k], right[c, pl.ds(k * bs, bs), :], preferred_element_type=F32)
    return total


def drop_absent(ref, pattern, row_device, column_device, rb, bs, panels=None):
    for r in range(rb):
        for j in range(rb if panels is None else panels):
            slot = slot_of(pattern, row_device * rb + r, column_device * rb + j)

            @pl.when(slot < 0)
            def _():
                ref[j, pl.ds(r * bs, bs), :] = jnp.zeros((bs, bs), ref.dtype)


def place(slots, held, cut, start, size):
    for j, slot in enumerate(slots):
        block = held[jnp.maximum(slot, 0)]
        cut[j, pl.ds(start, size), :] = jnp.where(slot >= 0, block, jnp.zeros_like(block))


def first_kernel(devices, rb, bs, pattern_hbm, blocks, cut, pattern, held, pattern_sem, sem):
    fetch = pltpu.make_async_copy(pattern_hbm, pattern, pattern_sem)
    fetch.start()
    load = pltpu.make_async_copy(blocks.at[0, :, pl.ds(0, bs // 2), :], held, sem)
    load.start()
    me, other, _ = neighbours(devices)
    fetch.wait()
    columns = [pattern[s, me * rb] - other * rb for s in range(pattern.shape[0])]
    slots = [jnp.int32(-1)] * rb
    for s, column in enumerate(columns):
        slots = [jnp.where(column == j, s, slot) for j, slot in enumerate(slots)]
    load.wait()
    place(slots, held, cut, 0, bs // 2)


def pack_kernel(devices, rb, bs, pattern_hbm, blocks, _, others, *rest):
    cuts, (pattern, held, pattern_sem, sems) = rest[:3], rest[3:]
    fetch = pltpu.make_async_copy(pattern_hbm, pattern, pattern_sem)
    fetch.start()
    loads = [pltpu.make_async_copy(blocks.at[r], held.at[r], sems.at[r]) for r in range(rb)]
    for load in loads:
        load.start()
    people = neighbours(devices)
    me, other, partner = people
    fetch.wait()
    for r in range(rb):
        loads[r].wait()
        for cut, columns in zip(cuts, (other, me, partner)):
            slots = [slot_of(pattern, me * rb + r, columns * rb + j) for j in range(rb)]
            place(slots, held.at[r], cut, r * bs, bs)
    others[...] = cuts[0][:, pl.ds(bs // 2, rb * bs - bs // 2), :]


def pack(devices, pattern, blocks):
    rb, slots, bs, _ = blocks.shape
    pattern = pltpu.with_memory_space_constraint(pattern, pltpu.HBM)
    blocks = pltpu.with_memory_space_constraint(blocks, pltpu.HBM)
    cut = lambda rows: jax.ShapeDtypeStruct((rb, rows, bs), blocks.dtype)
    params = pltpu.CompilerParams(vmem_limit_bytes=VMEM_LIMIT)
    first = pl.pallas_call(
        functools.partial(first_kernel, devices, rb, bs),
        out_shape=cut(bs // 2),
        in_specs=[ANY, ANY],
        out_specs=VMEM,
        scratch_shapes=[
            pltpu.SMEM(pattern.shape, pattern.dtype),
            pltpu.VMEM((slots, bs // 2, bs), blocks.dtype),
            pltpu.SemaphoreType.DMA,
            pltpu.SemaphoreType.DMA,
        ],
        compiler_params=params,
        cost_estimate=BRIEF,
        name="first",
    )(pattern, blocks)
    return first, *pl.pallas_call(
        functools.partial(pack_kernel, devices, rb, bs),
        out_shape=[cut(rb * bs - bs // 2)] + [cut(rb * bs)] * 3,
        in_specs=[ANY, ANY, ANY],
        out_specs=[VMEM] * 4,
        scratch_shapes=[
            pltpu.SMEM(pattern.shape, pattern.dtype),
            pltpu.VMEM(blocks.shape, blocks.dtype),
            pltpu.SemaphoreType.DMA,
            pltpu.SemaphoreType.DMA((rb,)),
        ],
        compiler_params=params,
        cost_estimate=BRIEF,
        name="pack",
    )(pattern, blocks, first)


def scatter(out, pattern, me, column_device, panels, j, sems, base, rb, bs):
    waits = []
    for r in range(rb):
        slot = slot_of(pattern, me * rb + r, column_device * rb + j)
        copy = pltpu.make_async_copy(
            panels.at[j, pl.ds(r * bs, bs), :], out.at[r, jnp.maximum(slot, 0)], sems.at[base + r * rb + j]
        )
        pl.when(slot >= 0)(copy.start)
        waits.append((slot, copy))
    return waits


def settle(waits):
    for slot, copy in waits:
        pl.when(slot >= 0)(copy.wait)


def begin_kernel(devices, rb, bs, outer, from_first, part):
    @pl.loop(0, rb)
    def _(c):
        part[c] = jnp.dot(outer[0, :, pl.ds(0, bs // 2)], from_first[c], preferred_element_type=F32)


def outer_kernel(devices, rb, bs, outer, from_first, from_others, part, from_outer, own_part):
    half = bs // 2
    from_outer[:, pl.ds(0, half), :] = from_first[...]
    from_outer[:, pl.ds(half, rb * bs - half), :] = from_others[...]

    @pl.loop(0, rb)
    def _(c):
        total = part[c] + jnp.dot(
            outer[0, :, pl.ds(half, half)], from_others[c, pl.ds(0, half), :], preferred_element_type=F32
        )
        for k in range(1, rb):
            rows = pl.ds(k * bs - half, bs)
            total += jnp.dot(outer[k], from_others[c, rows, :], preferred_element_type=F32)
        own_part[c] = total


def square_kernel(devices, rb, bs, pattern, own, inner, from_inner, own_part, s_own, s_head):
    me, _, _ = neighbours(devices)

    @pl.loop(0, rb)
    def _(c):
        s_own[c] = (
            own_part[c] + panel_product(own, own, c, rb, bs) + panel_product(inner, from_inner, c, rb, bs)
        ).astype(BF16)

    drop_absent(s_own, pattern, me, me, rb, bs)
    s_head[...] = s_own[pl.ds(0, rb - 1)]


def early_kernel(
    devices, rb, bs, pattern, own, inner, outer, from_inner, inner_own, from_outer, s_own,
    cube_part, inner_part, from_outer_part, outer_part, s_inner, s_from_inner, sems,
):
    me, _, partner = neighbours(devices)

    @pl.loop(0, rb)
    def _(c):
        s_inner[c] = (panel_product(own, inner, c, rb, bs) + panel_product(inner, inner_own, c, rb, bs)).astype(BF16)
        s_from_inner[c] = (
            panel_product(from_inner, own, c, rb, bs) + panel_product(inner_own, from_inner, c, rb, bs)
        ).astype(BF16)
        from_outer_part[c] = panel_product(from_outer, own, c, rb, bs)
        outer_part[c] = panel_product(own, outer, c, rb, bs)

    drop_absent(s_inner, pattern, me, partner, rb, bs)
    drop_absent(s_from_inner, pattern, partner, me, rb, bs)

    @pl.loop(0, rb)
    def _(c):
        cube_part[c] = panel_product(own, s_own, c, rb, bs) + panel_product(inner, s_from_inner, c, rb, bs)
        inner_part[c] = 3.0 * s_inner[c].astype(F32) - 2.0 * panel_product(own, s_inner, c, rb, bs)


def ahead_kernel(
    devices, rb, bs, pattern, outer_own, from_outer, from_outer_part, s_own, s_from_outer, out_most, out_last, slots
):
    me, other, _ = neighbours(devices)
    last = rb - 1
    for r in range(rb):
        slots[r] = jnp.full(slots.shape[1:], slot_of(pattern, me * rb + r, other * rb + last))

    @pl.loop(0, rb)
    def _(c):
        s_from_outer[c] = (from_outer_part[c] + panel_product(outer_own, from_outer, c, rb, bs)).astype(BF16)

    drop_absent(s_from_outer, pattern, other, me, rb, bs)
    cube = panel_product(outer_own, s_from_outer, last, rb, bs) + panel_product(from_outer, s_own, last, rb, bs)
    out_there = (3.0 * s_from_outer[last].astype(F32) - 2.0 * cube).astype(BF16)
    out_most[...] = out_there[: last * bs]
    out_last[...] = out_there[last * bs :]


def late_kernel(
    devices, rb, bs, pattern, own, outer, outer_own, s_from_outer, s_own, outer_part, cube_part, inner,
    s_inner_own, inner_part, out, rest, s_outer, out_own, out_inner, sems,
):
    me, other, partner = neighbours(devices)
    waits = []
    for c in range(rb):
        out_inner[c] = (inner_part[c] - 2.0 * panel_product(inner, s_inner_own, c, rb, bs)).astype(BF16)
        waits += scatter(out, pattern, me, partner, out_inner, c, sems, rb * rb, rb, bs)
    for c in range(rb):
        cube = cube_part[c] + panel_product(outer, s_from_outer, c, rb, bs)
        out_own[c] = (3.0 * s_own[c].astype(F32) - 2.0 * cube).astype(BF16)
        waits += scatter(out, pattern, me, me, out_own, c, sems, 0, rb, bs)

    @pl.loop(0, rb - 1)
    def _(c):
        s_outer[c] = (outer_part[c] + panel_product(outer, outer_own, c, rb, bs)).astype(BF16)

    drop_absent(s_outer, pattern, me, other, rb, bs, rb - 1)

    @pl.loop(0, rb - 1)
    def _(c):
        rest[c] = 3.0 * s_outer[c].astype(F32) - 2.0 * panel_product(own, s_outer, c, rb, bs)

    settle(waits)


def head_kernel(devices, rb, bs, pattern, outer, s_outer_head, rest, _, out, out_outer, sems):
    me, other, _ = neighbours(devices)
    waits = []
    for c in range(rb - 1):
        out_outer[c] = (rest[c] - 2.0 * panel_product(outer, s_outer_head, c, rb, bs)).astype(BF16)
        waits += scatter(out, pattern, me, other, out_outer, c, sems, 0, rb, bs)
    settle(waits)


def tail_kernel(first, bs, slots, blocks, _, out, sems):
    waits = []
    for r in range(blocks.shape[0] // bs):
        slot = slots[first + r, 0, 0]
        copy = pltpu.make_async_copy(
            blocks.at[pl.ds(r * bs, bs), :], out.at[first + r, jnp.maximum(slot, 0)], sems.at[r]
        )
        pl.when(slot >= 0)(copy.start)
        waits.append((slot, copy))
    settle(waits)


def local(devices, block_values, pattern):
    rb, _, bs, _ = block_values.shape
    pattern = pattern.T
    over = [(i, (i + 1 if i % 2 else i - 1) % devices) for i in range(devices)]
    across = [(i, i ^ 1) for i in range(devices)]
    to_outer = lambda x: lax.ppermute(x, "grid", over)
    to_inner = lambda x: lax.ppermute(x, "grid", across)
    low_of = lambda panels: jax.ShapeDtypeStruct((panels, rb * bs, bs), BF16)
    low = low_of(rb)
    high = jax.ShapeDtypeStruct(low.shape, F32)
    full = jax.ShapeDtypeStruct(block_values.shape, BF16)

    def call(kernel, operands, outs, scratch=(), into=None, patterned=True, cost=BRIEF):
        in_specs = [VMEM] * len(operands)
        if patterned:
            operands = (pltpu.with_memory_space_constraint(pattern, pltpu.SMEM), *operands)
            in_specs = [SMEM] + in_specs
        aliases = {}
        if into is not None:
            aliases = {len(operands): 0}
            operands, in_specs = (*operands, into), in_specs + [ANY]
        scratch = [pltpu.VMEM(low.shape, BF16)] * scratch + [pltpu.SemaphoreType.DMA((2 * rb * rb,))] if scratch else []
        return pl.pallas_call(
            functools.partial(kernel, devices, rb, bs),
            out_shape=outs,
            in_specs=in_specs,
            out_specs=[ANY if out is full else VMEM for out in outs],
            scratch_shapes=scratch,
            input_output_aliases=aliases,
            compiler_params=pltpu.CompilerParams(vmem_limit_bytes=VMEM_LIMIT),
            cost_estimate=cost,
            name=kernel.__name__,
        )(*operands)

    first, others, outer, own, inner = pack(devices, pattern, block_values)
    from_first, from_others = to_outer(first), to_outer(others)
    outer_own = to_outer(own)
    from_inner, inner_own = to_inner(inner), to_inner(own)

    (part,) = call(begin_kernel, (outer, from_first), (high,), patterned=False, cost=LONGEST)
    from_outer, own_part = call(outer_kernel, (outer, from_first, from_others, part), (low, high), patterned=False, cost=LONGER)
    s_own, s_head = call(square_kernel, (own, inner, from_inner, own_part), (low, low_of(rb - 1)))
    s_outer_head = to_outer(s_head)
    s_inner_own = to_inner(s_own)
    cube_part, inner_part, from_outer_part, outer_part = call(
        early_kernel, (own, inner, outer, from_inner, inner_own, from_outer, s_own), (high,) * 4, 2
    )
    s_from_outer, out_most, out_last, slots = call(
        ahead_kernel,
        (outer_own, from_outer, from_outer_part, s_own),
        (
            low,
            jax.ShapeDtypeStruct(((rb - 1) * bs, bs), BF16),
            jax.ShapeDtypeStruct((bs, bs), BF16),
            jax.ShapeDtypeStruct((rb, 8, 128), jnp.int32),
        ),
        cost=BRIEF,
    )
    arrivals = to_outer(out_most), to_outer(out_last)
    out, rest = call(
        late_kernel,
        (own, outer, outer_own, s_from_outer, s_own, outer_part, cube_part, inner, s_inner_own, inner_part),
        (full, high),
        3,
        cost=BRIEF,
    )
    (out,) = call(head_kernel, (outer, s_outer_head, rest), (full,), 1, into=out, cost=BRIEF)
    for first, blocks in zip((0, rb - 1), arrivals):
        out = pl.pallas_call(
            functools.partial(tail_kernel, first, bs),
            out_shape=full,
            in_specs=[VMEM, VMEM, ANY],
            out_specs=ANY,
            scratch_shapes=[pltpu.SemaphoreType.DMA((blocks.shape[0] // bs,))],
            input_output_aliases={2: 0},
            compiler_params=pltpu.CompilerParams(vmem_limit_bytes=VMEM_LIMIT),
            cost_estimate=BRIEF,
            name="tail_kernel",
        )(slots, blocks, out)
    return out


def solution(mesh):
    return jax.shard_map(
        functools.partial(local, mesh.shape["grid"]),
        mesh=mesh,
        in_specs=(P(("parts", "grid"), None, None, None), P("parts", None)),
        out_specs=P(("parts", "grid"), None, None, None),
        check_vma=False,
    )
```
